32 devices in a mesh: clip: 2 (over y), frames: 4 (over z), rows: 2 (over x), heads: 2 (over core).
Axes of the slice: x: 2, y: 2, z: 4, core: 2. Of those that a mesh axis runs over, the one named last changes fastest.
Arguments:
- tok_q: bfloat16 [64, 32, 1536], P(('clip', 'frames'), 'rows', 'heads'), parts along dimension 0, may hold values from -125 to 125, as said below
- tok_kv: bfloat16 [2, 64, 32, 1536], P(None, ('clip', 'frames'), 'rows', 'heads'), parts along dimension 1, may hold values from -6 to 6
- ref_kv: bfloat16 [2, 4, 768, 1536], P(None, 'clip', ('frames', 'rows'), 'heads'), parts along dimension 1, may hold values from -6 to 6
- ref_ids: int32 [64], P(('clip', 'frames')), parts along dimension 0, may hold values from 0 to 1
Outputs:
- mixed: bfloat16 [64, 32, 1536], P(('clip', 'frames'), 'rows', 'heads'), parts along dimension 0
The draws below stay inside these ranges and needn't reach their ends.
There are 2 independent parts, one for each index of `clip`. The reference program is written for one: setup_inputs(seed, part) draws one part's arguments, and reference() takes and returns one part's arrays. A program takes and returns all parts, laid end to end along the dimension named above; each array names one. Nothing has to cross between parts.
Inputs may be any that keep to these rules, and one draw needn't show every extreme that they name: `tok_q`: queries of the clip's tokens.
All inputs are finite; a program needn't handle non-finite values.
Results may differ from the reference program's by a relative error of at most 0.0048.
Values may be sent and summed in bfloat16 or wider, within the bound.
A program may use at most 64 MiB of HBM per device.

```python
import jax
import jax.numpy as jnp
from jax import lax

HEADS = 12
HEAD_DIM = 128
BAND = 8
NREF = 2
REF_TOK = 768
WIDTH = 1536
FRAMES = 32
TOK = 32


def token_fields(key):
    base = jax.random.fold_in(key, 11)
    seed_query, seed_keys, seed_values = jax.random.split(base, 3)
    shape = (FRAMES, TOK, HEADS * HEAD_DIM)
    query = 2.0 * jnp.clip(jax.random.normal(seed_query, shape, jnp.float32), -6.0, 6.0)
    keys_raw = jnp.clip(jax.random.normal(seed_keys, shape, jnp.float32), -5.0, 5.0)
    values = jnp.clip(jax.random.normal(seed_values, shape, jnp.float32), -6.0, 6.0)
    return (query, jnp.stack([keys_raw, values]))


def draw_tok_q(key, part):
    return token_fields(key)[0].astype(jnp.bfloat16)


def draw_tok_kv(key, part):
    return token_fields(key)[1].astype(jnp.bfloat16)


def set_ends(result, key, least, high):
    longest = result.shape.index(max(result.shape))
    spots = []
    for shift in (0, 1):
        where = [jax.random.randint(jax.random.fold_in(key, axis), (), 0, length) for axis, length in enumerate(result.shape)]
        where[longest] = (where[longest] + shift) % result.shape[longest]
        spots.append(tuple(where))
    return result.at[spots[0]].set(least).at[spots[1]].set(high)


def shard_levels(stream_key, dims, shards, low, high):
    level, own = 1.0, jax.random.fold_in(stream_key, 6)
    for dim, shards_of in shards:
        draws = jnp.exp(jax.random.uniform(jax.random.fold_in(own, dim), (shards_of,), jnp.float32, low / len(shards), high / len(shards)))
        level = level * jnp.repeat(draws, dims[dim] // shards_of).reshape([-1 if axis == dim else 1 for axis in range(len(dims))])
    return level


def normal_values(rng, extent, scale, bound, cuts=(), held_as=jnp.bfloat16):
    loudness = shard_levels(rng, extent, cuts, -0.22, 0.18) if cuts else 1.0
    drawn = jax.random.normal(rng, extent, jnp.float32) * scale * loudness
    return jnp.minimum(jnp.maximum(drawn, -bound), bound).astype(held_as)


def setup_inputs(seed: int = 0, part: int = 0) -> dict:
    key_of = jax.random.split(jax.random.key(seed), 5)
    own_keys = jax.random.split(jax.random.fold_in(key_of[4], part), 5)
    return {
        "tok_q": draw_tok_q(jax.random.fold_in(jax.random.fold_in(key_of[4], part), 71), part),
        "tok_kv": draw_tok_kv(jax.random.fold_in(jax.random.fold_in(key_of[4], part), 71), part),
        "ref_kv": normal_values(own_keys[2], (2, NREF, REF_TOK, WIDTH), 1.0, 6.0, ((2, 8), (3, 2))),
        "ref_ids": set_ends(jax.random.randint(own_keys[3], (FRAMES,), 0, NREF), jax.random.fold_in(own_keys[3], 1), 0, NREF - 1).astype(jnp.int32),
    }


def reference(tok_q, tok_kv, ref_kv, ref_ids):
    frame_total = tok_q.shape[0]
    factor = 1.0 / (HEAD_DIM ** 0.5)
    offsets = jnp.arange(-BAND, BAND + 1, dtype=jnp.int32)

    def one_frame(frame):
        query = tok_q[frame].astype(jnp.float32).reshape(TOK, HEADS, HEAD_DIM)
        window = ((frame + offsets) % frame_total).astype(jnp.int32)
        band_keys = jnp.take(tok_kv[0], window, axis=0).astype(jnp.float32).reshape(2 * BAND + 1, TOK, HEADS, HEAD_DIM)
        band_values = jnp.take(tok_kv[1], window, axis=0).astype(jnp.float32).reshape(2 * BAND + 1, TOK, HEADS, HEAD_DIM)
        band_scores = jnp.einsum('thd,othd->oth', query, band_keys) * factor
        band_weights = lax.optimization_barrier(jax.nn.softmax(band_scores, axis=0).astype(jnp.bfloat16)).astype(jnp.float32)
        temporal = jnp.einsum('oth,othd->thd', band_weights, band_values)
        frame_keys = tok_kv[0, frame].astype(jnp.float32).reshape(TOK, HEADS, HEAD_DIM)
        frame_values = tok_kv[1, frame].astype(jnp.float32).reshape(TOK, HEADS, HEAD_DIM)
        chosen = jnp.take(ref_kv, ref_ids[frame], axis=1)
        image_keys = chosen[0].astype(jnp.float32).reshape(REF_TOK, HEADS, HEAD_DIM)
        image_values = chosen[1].astype(jnp.float32).reshape(REF_TOK, HEADS, HEAD_DIM)
        local_scores = jnp.einsum('thd,shd->hts', query, frame_keys) * factor
        image_scores = jnp.einsum('thd,shd->hts', query, image_keys) * factor
        top = jnp.maximum(jnp.max(local_scores, axis=-1), jnp.max(image_scores, axis=-1))
        local_exp = jnp.exp(local_scores - top[..., None])
        image_exp = jnp.exp(image_scores - top[..., None])
        total = jnp.sum(local_exp, axis=-1) + jnp.sum(image_exp, axis=-1)
        local_weights = lax.optimization_barrier((local_exp / total[..., None]).astype(jnp.bfloat16)).astype(jnp.float32)
        image_weights = lax.optimization_barrier((image_exp / total[..., None]).astype(jnp.bfloat16)).astype(jnp.float32)
        spatial = jnp.einsum('hts,shd->thd', local_weights, frame_values) + jnp.einsum('hts,shd->thd', image_weights, image_values)
        return (temporal + spatial).reshape(TOK, HEADS * HEAD_DIM).astype(jnp.bfloat16)

    return lax.map(one_frame, jnp.arange(frame_total, dtype=jnp.int32))
```

```python
import functools

import jax
import jax.numpy as jnp
from jax import lax
from jax.experimental import pallas as pl
from jax.experimental.pallas import tpu as pltpu
from jax.sharding import PartitionSpec as P

HEAD_DIM = 128
BAND = 8


def padded_2(value, sides, width):
    for axis, dim in sides:
        devices, length = (lax.axis_size(axis), value.shape[dim])
        up = [(i, (i + 1) % devices) for i in range(devices)]
        down = [(j, i) for i, j in up]
        last = lax.slice_in_dim(value, length - width, length, axis=dim)
        first = lax.slice_in_dim(value, 0, width, axis=dim)
        before = lax.ppermute(last, axis, up)
        after = lax.ppermute(first, axis, down)
        value = jnp.concatenate([before, value, after], axis=dim)
    return value


def attend_frame(query, frame_keys, frame_values, image_keys, image_values, factor):
    local_scores = (
        jnp.einsum("thd,shd->hts", query, frame_keys, preferred_element_type=jnp.float32) * factor
    )
    image_scores = (
        jnp.einsum("thd,shd->hts", query, image_keys, preferred_element_type=jnp.float32) * factor
    )
    top = jnp.maximum(jnp.max(local_scores, axis=-1), jnp.max(image_scores, axis=-1))
    local_exp = jnp.exp(local_scores - top[..., None])
    image_exp = jnp.exp(image_scores - top[..., None])
    total = jnp.sum(local_exp, axis=-1) + jnp.sum(image_exp, axis=-1)
    local_weights = (local_exp / total[..., None]).astype(jnp.bfloat16)
    image_weights = (image_exp / total[..., None]).astype(jnp.bfloat16)
    result = jnp.einsum(
        "hts,shd->thd", local_weights, frame_values, preferred_element_type=jnp.float32
    )
    result = result + jnp.einsum(
        "hts,shd->thd", image_weights, image_values, preferred_element_type=jnp.float32
    )
    return result


def local_general(tok_q, tok_kv, ref_kv, ref_ids):
    frame_count, row_count, feat_width = tok_q.shape
    head_count = feat_width // HEAD_DIM
    factor = 1.0 / HEAD_DIM**0.5
    query_heads = tok_q.reshape(frame_count, row_count, head_count, HEAD_DIM)
    padded = padded_2(tok_kv, (("frames", 1),), BAND)
    band_scores = []
    for offset in range(2 * BAND + 1):
        key_block = padded[0, offset : offset + frame_count].reshape(
            frame_count, row_count, head_count, HEAD_DIM
        )
        band_scores.append(
            jnp.einsum("frhd,frhd->frh", query_heads, key_block, preferred_element_type=jnp.float32)
            * factor
        )
    band_weights = jax.nn.softmax(jnp.stack(band_scores), axis=0).astype(jnp.bfloat16)
    temporal = jnp.zeros((frame_count, row_count, head_count, HEAD_DIM), jnp.float32)
    for offset in range(2 * BAND + 1):
        value_block = padded[1, offset : offset + frame_count].reshape(
            frame_count, row_count, head_count, HEAD_DIM
        )
        temporal = temporal + jnp.einsum(
            "frh,frhd->frhd", band_weights[offset], value_block, preferred_element_type=jnp.float32
        )
    temporal = temporal.reshape(frame_count, row_count, feat_width)
    references = lax.all_gather(ref_kv, ("frames", "rows"), axis=2, tiled=True)
    ref_length = references.shape[2]

    def spatial_frame(inputs):
        query_frame, keys_frame, values_frame, image_id = inputs
        chosen = lax.dynamic_index_in_dim(references, image_id, axis=1, keepdims=False)
        image_keys = chosen[0].reshape(ref_length, head_count, HEAD_DIM)
        image_values = chosen[1].reshape(ref_length, head_count, HEAD_DIM)
        queries = query_frame.reshape(query_frame.shape[0], head_count, HEAD_DIM)
        keys_full = keys_frame.reshape(keys_frame.shape[0], head_count, HEAD_DIM)
        values_full = values_frame.reshape(values_frame.shape[0], head_count, HEAD_DIM)
        result = attend_frame(queries, keys_full, values_full, image_keys, image_values, factor)
        return result.reshape(query_frame.shape[0], feat_width)

    query_moved, pairs_moved = (
        lax.all_to_all(tok_q[None], "rows", split_axis=1, concat_axis=2, tiled=True),
        lax.all_to_all(tok_kv, "rows", split_axis=1, concat_axis=2, tiled=True),
    )
    per_device = frame_count // lax.axis_size("rows")
    local_ids = lax.dynamic_slice_in_dim(ref_ids, lax.axis_index("rows") * per_device, per_device)
    attended = lax.map(spatial_frame, (query_moved[0], pairs_moved[0], pairs_moved[1], local_ids))
    spatial = lax.all_to_all(attended, "rows", split_axis=1, concat_axis=0, tiled=True)
    return (temporal + spatial).astype(jnp.bfloat16)


NEG = -1e30
MESH = pl.DeviceIdType.MESH


def scores_of(keys, queries):
    return lax.dot_general(
        keys, queries, (((1,), (1,)), ((), ())), preferred_element_type=jnp.float32
    )


def kernel(
    n,
    q_hbm,
    kv_hbm,
    ref_hbm,
    ids_ref,
    out_ref,
    qbuf,
    kvbuf,
    rbuf,
    idbuf,
    pref,
    ptime,
    pframe,
    stats,
    vt,
    own,
    part,
    got,
    local_sem,
    xs_sem,
    xr_sem,
    qs_sem,
    qr_sem,
    is_sem,
    ir_sem,
    ss_sem,
    sr_sem,
    ps_sem,
    pr_sem,
):
    frame_count, row_count, width = q_hbm.shape
    head_count = width // HEAD_DIM
    tokens = frame_count * row_count
    images, ref_rows = ref_hbm.shape[1], ref_hbm.shape[2]
    span = 2 * ref_rows
    factor = 1.0 / HEAD_DIM**0.5
    me = lax.axis_index("frames")
    across = {"rows": 1 - lax.axis_index("rows")}
    ahead = [{"frames": lax.rem(me + d, n)} for d in range(n)]
    behind = [{"frames": lax.rem(me + n - d, n)} for d in range(n)]
    banded = (0, 1, n - 1)
    order = [0, 1, n - 1] + list(range(2, n - 1))

    loads = [
        pltpu.make_async_copy(q_hbm, qbuf.at[0], local_sem.at[0]),
        pltpu.make_async_copy(ref_hbm.at[0], rbuf.at[0, :, pl.ds(0, ref_rows)], local_sem.at[1]),
        pltpu.make_async_copy(kv_hbm, kvbuf.at[0], local_sem.at[2]),
        pltpu.make_async_copy(ref_hbm.at[1], rbuf.at[1, :, pl.ds(0, ref_rows)], local_sem.at[3]),
    ]
    for copy in loads:
        copy.start()

    barrier = pltpu.get_barrier_semaphore()
    for d in range(1, n):
        pl.semaphore_signal(barrier, inc=1, device_id=ahead[d], device_id_type=MESH)
    pl.semaphore_signal(barrier, inc=1, device_id=across, device_id_type=MESH)

    lane_frame = lax.broadcasted_iota(jnp.int32, (8, tokens), 1) // row_count
    which = jnp.zeros((8, tokens), jnp.int32)
    for f in range(frame_count):
        which = jnp.where(lane_frame == f, ids_ref[f], which)
    idbuf[0] = which

    pl.semaphore_wait(barrier, n)

    def remote(src, dst, send, recv, where):
        return pltpu.make_async_remote_copy(
            src_ref=src, dst_ref=dst, send_sem=send, recv_sem=recv,
            device_id=where, device_id_type=MESH,
        )

    far = pl.ds(ref_rows, ref_rows)
    xcopies = [
        remote(ref_hbm.at[0], rbuf.at[0, :, far], xs_sem.at[0], xr_sem.at[0], across),
        remote(kv_hbm.at[0], kvbuf.at[1, 0], xs_sem.at[1], xr_sem.at[1], across),
        remote(ref_hbm.at[1], rbuf.at[1, :, far], xs_sem.at[2], xr_sem.at[2], across),
        remote(kv_hbm.at[1], kvbuf.at[1, 1], xs_sem.at[3], xr_sem.at[3], across),
    ]
    qcopies = [None] + [
        remote(q_hbm, qbuf.at[d], qs_sem.at[d], qr_sem.at[d], ahead[d]) for d in range(1, n)
    ]
    icopies = [None] + [
        remote(idbuf.at[0], idbuf.at[d], is_sem.at[d], ir_sem.at[d], ahead[d]) for d in range(1, n)
    ]
    for copy in icopies[1:]:
        copy.start()
    xcopies[0].start()
    for d in order[1:]:
        qcopies[d].start()
    for copy in xcopies[1:]:
        copy.start()

    def lanes(h):
        return pl.ds(pl.multiple_of(h * HEAD_DIM, HEAD_DIM), HEAD_DIM)

    row = lax.broadcasted_iota(jnp.int32, (tokens, tokens), 0)
    col = lax.broadcasted_iota(jnp.int32, (tokens, tokens), 1)
    key_frame, key_row = row // row_count, row % row_count
    query_frame, query_row = col // row_count, col % row_count
    same_frame = key_frame == query_frame

    def in_band(d):
        mask = key_row == query_row
        if d == 1:
            mask = mask & (key_frame <= query_frame)
        elif d == n - 1:
            mask = mask & (key_frame >= query_frame)
        return mask

    def score_block(d):
        mask = in_band(d) if d in banded else None

        def body(h):
            cut = lanes(h)
            query = qbuf[d, :, :, cut].reshape(tokens, HEAD_DIM)
            image_keys = rbuf[0, :, :, cut].reshape(images * span, HEAD_DIM)
            both = scores_of(image_keys, query)
            chosen = idbuf[d][0:1]
            score = both[0:span]
            for i in range(1, images):
                score = jnp.where(chosen == i, both[i * span : (i + 1) * span], score)
            score = score * factor
            top = jnp.max(score, axis=0, keepdims=True)
            zero = jnp.zeros_like(top)
            time_top, time_sum = zero, zero
            if d in banded:
                keys = kvbuf[0, 0, :, :, cut].reshape(tokens, HEAD_DIM)
                near = scores_of(keys, query) * factor
                time_score = jnp.where(mask, near, NEG)
                time_top = jnp.max(time_score, axis=0, keepdims=True)
                time_exp = jnp.exp(time_score - time_top)
                time_sum = jnp.sum(time_exp, axis=0, keepdims=True)
                ptime[d, h] = time_exp
            if d == 0:
                other_keys = kvbuf[1, 0, :, :, cut].reshape(tokens, HEAD_DIM)
                other = scores_of(other_keys, query) * factor
                near = jnp.where(same_frame, near, NEG)
                other = jnp.where(same_frame, other, NEG)
                top = jnp.maximum(top, jnp.max(near, axis=0, keepdims=True))
                top = jnp.maximum(top, jnp.max(other, axis=0, keepdims=True))
                near = jnp.exp(near - top)
                other = jnp.exp(other - top)
                pframe[h, 0] = near
                pframe[h, 1] = other
            score = jnp.exp(score - top)
            total = jnp.sum(score, axis=0, keepdims=True)
            if d == 0:
                total = total + jnp.sum(near, axis=0, keepdims=True)
                total = total + jnp.sum(other, axis=0, keepdims=True)
            pref[d, h] = score
            stats[0, d, h] = jnp.concatenate([top, total, time_top, time_sum], axis=0)

        return body

    def each_head(body):
        def pair(i, carry):
            body(2 * i)
            body(2 * i + 1)
            return carry

        lax.fori_loop(0, head_count // 2, pair, 0)

    def scale_of(d, h, k):
        tops, sums = [], []
        for e in range(n):
            place = (d - e) % n
            if k == 2 and place not in banded:
                continue
            block = stats[e, place, h]
            tops.append(block[k : k + 1])
            sums.append(block[k + 1 : k + 2])
        top = functools.reduce(jnp.maximum, tops)
        total = sum(s * jnp.exp(t - top) for t, s in zip(tops, sums))
        return jnp.exp(tops[0] - top) / total

    def value_block(d):
        def body(h):
            chosen = idbuf[d][0:1]
            weight = pref[d, h] * scale_of(d, h, 0)
            weights = [
                jnp.where(chosen == i, weight, 0.0).astype(jnp.bfloat16) for i in range(images)
            ]
            if d in banded:
                weights.append((ptime[d, h] * scale_of(d, h, 2)).astype(jnp.bfloat16))
            weight = jnp.concatenate(weights, axis=0)
            values = vt[h, :, 0 : weight.shape[0]]
            result = jnp.dot(values, weight, preferred_element_type=jnp.float32)
            if d == 0:
                scale = scale_of(d, h, 0)
                for i in range(2):
                    start = images * span + i * tokens
                    result = result + jnp.dot(
                        vt[h, :, start : start + tokens],
                        (pframe[h, i] * scale).astype(jnp.bfloat16),
                        preferred_element_type=jnp.float32,
                    )
                own[h] = result
            else:
                part[d, h] = result.astype(jnp.bfloat16)

        return body

    def turn_values(h):
        cut = lanes(h)
        blocks = [
            rbuf[1, :, :, cut].reshape(images * span, HEAD_DIM),
            kvbuf[0, 1, :, :, cut].reshape(tokens, HEAD_DIM),
            kvbuf[1, 1, :, :, cut].reshape(tokens, HEAD_DIM),
        ]
        values = jnp.concatenate(blocks, axis=0).astype(jnp.float32)
        vt[h] = values.T.astype(jnp.bfloat16)

    for copy in loads:
        copy.wait()
    xcopies[0].wait_recv()
    xcopies[1].wait_recv()
    each_head(score_block(0))
    for d in order[1:]:
        icopies[d].wait_recv()
        qcopies[d].wait_recv()
        each_head(score_block(d))
    scopies = [None] + [
        remote(stats.at[0], stats.at[d], ss_sem.at[d], sr_sem.at[d], ahead[d])
        for d in range(1, n)
    ]
    for copy in scopies[1:]:
        copy.start()
    xcopies[2].wait_recv()
    xcopies[3].wait_recv()
    each_head(turn_values)
    for copy in scopies[1:]:
        copy.wait_recv()
    pcopies = [None] + [
        remote(part.at[d], got.at[d], ps_sem.at[d], pr_sem.at[d], behind[d]) for d in range(1, n)
    ]
    for d in order[:0:-1]:
        each_head(value_block(d))
        pcopies[d].start()
    each_head(value_block(0))
    for copy in pcopies[1:]:
        copy.wait_recv()

    def finish(h):
        total = own[h]
        for d in range(1, n):
            total = total + got[d, h].astype(jnp.float32)
        out_ref[:, :, lanes(h)] = total.T.reshape(frame_count, row_count, HEAD_DIM).astype(
            jnp.bfloat16
        )

    each_head(finish)
    for copies in (xcopies, qcopies[1:], icopies[1:], scopies[1:], pcopies[1:]):
        for copy in copies:
            copy.wait_send()


def local_kernel(tok_q, tok_kv, ref_kv, ref_ids):
    n = lax.axis_size("frames")
    frame_count, row_count, width = tok_q.shape
    heads = width // HEAD_DIM
    tokens = frame_count * row_count
    images, ref_rows = ref_kv.shape[1:3]
    span = 2 * ref_rows
    dma = pltpu.SemaphoreType.DMA
    anywhere = pl.BlockSpec(memory_space=pl.ANY)
    return pl.pallas_call(
        functools.partial(kernel, n),
        out_shape=jax.ShapeDtypeStruct(tok_q.shape, jnp.bfloat16),
        in_specs=[anywhere] * 3 + [pl.BlockSpec(memory_space=pltpu.SMEM)],
        out_specs=pl.BlockSpec(memory_space=pltpu.VMEM),
        scratch_shapes=[
            pltpu.VMEM((n,) + tok_q.shape, jnp.bfloat16),
            pltpu.VMEM((2,) + tok_kv.shape, jnp.bfloat16),
            pltpu.VMEM((2, images, span, width), jnp.bfloat16),
            pltpu.VMEM((n, 8, tokens), jnp.int32),
            pltpu.VMEM((n, heads, span, tokens), jnp.float32),
            pltpu.VMEM((n, heads, tokens, tokens), jnp.float32),
            pltpu.VMEM((heads, 2, tokens, tokens), jnp.float32),
            pltpu.VMEM((n, n, heads, 4, tokens), jnp.float32),
            pltpu.VMEM((heads, HEAD_DIM, images * span + 2 * tokens), jnp.bfloat16),
            pltpu.VMEM((heads, HEAD_DIM, tokens), jnp.float32),
            pltpu.VMEM((n, heads, HEAD_DIM, tokens), jnp.bfloat16),
            pltpu.VMEM((n, heads, HEAD_DIM, tokens), jnp.bfloat16),
            dma((4,)),
            dma((4,)),
            dma((4,)),
        ]
        + [dma((n,))] * 8,
        compiler_params=pltpu.CompilerParams(
            collective_id=0, has_side_effects=True, vmem_limit_bytes=48 * 1024 * 1024
        ),
    )(tok_q, tok_kv, ref_kv, ref_ids)


def local(tok_q, tok_kv, ref_kv, ref_ids):
    frame_count, row_count, width = tok_q.shape
    fits = (
        3 <= lax.axis_size("frames") <= 8
        and lax.axis_size("rows") == 2
        and frame_count == BAND
        and row_count % 16 == 0
        and frame_count * row_count == 128
        and ref_kv.shape[2] % 16 == 0
        and (width // HEAD_DIM) % 2 == 0
    )
    return (local_kernel if fits else local_general)(tok_q, tok_kv, ref_kv, ref_ids)


def solution(mesh):
    placed = (
        P(("clip", "frames"), "rows", "heads"),
        P(None, ("clip", "frames"), "rows", "heads"),
        P(None, "clip", ("frames", "rows"), "heads"),
        P(("clip", "frames")),
    )
    return jax.shard_map(
        local,
        mesh=mesh,
        in_specs=placed,
        out_specs=P(("clip", "frames"), "rows", "heads"),
        check_vma=False,
    )
```

```python
import functools

import jax
import jax.numpy as jnp
from jax import lax
from jax.experimental import pallas as pl
from jax.experimental.pallas import tpu as pltpu
from jax.sharding import PartitionSpec as P

HEAD_DIM = 128
BAND = 8


def padded_2(value, sides, width):
    for axis, dim in sides:
        devices, length = (lax.axis_size(axis), value.shape[dim])
        up = [(i, (i + 1) % devices) for i in range(devices)]
        down = [(j, i) for i, j in up]
        last = lax.slice_in_dim(value, length - width, length, axis=dim)
        first = lax.slice_in_dim(value, 0, width, axis=dim)
        before = lax.ppermute(last, axis, up)
        after = lax.ppermute(first, axis, down)
        value = jnp.concatenate([before, value, after], axis=dim)
    return value


def attend_frame(query, frame_keys, frame_values, image_keys, image_values, factor):
    local_scores = (
        jnp.einsum("thd,shd->hts", query, frame_keys, preferred_element_type=jnp.float32) * factor
    )
    image_scores = (
        jnp.einsum("thd,shd->hts", query, image_keys, preferred_element_type=jnp.float32) * factor
    )
    top = jnp.maximum(jnp.max(local_scores, axis=-1), jnp.max(image_scores, axis=-1))
    local_exp = jnp.exp(local_scores - top[..., None])
    image_exp = jnp.exp(image_scores - top[..., None])
    total = jnp.sum(local_exp, axis=-1) + jnp.sum(image_exp, axis=-1)
    local_weights = (local_exp / total[..., None]).astype(jnp.bfloat16)
    image_weights = (image_exp / total[..., None]).astype(jnp.bfloat16)
    result = jnp.einsum(
        "hts,shd->thd", local_weights, frame_values, preferred_element_type=jnp.float32
    )
    result = result + jnp.einsum(
        "hts,shd->thd", image_weights, image_values, preferred_element_type=jnp.float32
    )
    return result


def local_general(tok_q, tok_kv, ref_kv, ref_ids):
    frame_count, row_count, feat_width = tok_q.shape
    head_count = feat_width // HEAD_DIM
    factor = 1.0 / HEAD_DIM**0.5
    query_heads = tok_q.reshape(frame_count, row_count, head_count, HEAD_DIM)
    padded = padded_2(tok_kv, (("frames", 1),), BAND)
    band_scores = []
    for offset in range(2 * BAND + 1):
        key_block = padded[0, offset : offset + frame_count].reshape(
            frame_count, row_count, head_count, HEAD_DIM
        )
        band_scores.append(
            jnp.einsum("frhd,frhd->frh", query_heads, key_block, preferred_element_type=jnp.float32)
            * factor
        )
    band_weights = jax.nn.softmax(jnp.stack(band_scores), axis=0).astype(jnp.bfloat16)
    temporal = jnp.zeros((frame_count, row_count, head_count, HEAD_DIM), jnp.float32)
    for offset in range(2 * BAND + 1):
        value_block = padded[1, offset : offset + frame_count].reshape(
            frame_count, row_count, head_count, HEAD_DIM
        )
        temporal = temporal + jnp.einsum(
            "frh,frhd->frhd", band_weights[offset], value_block, preferred_element_type=jnp.float32
        )
    temporal = temporal.reshape(frame_count, row_count, feat_width)
    references = lax.all_gather(ref_kv, ("frames", "rows"), axis=2, tiled=True)
    ref_length = references.shape[2]

    def spatial_frame(inputs):
        query_frame, keys_frame, values_frame, image_id = inputs
        chosen = lax.dynamic_index_in_dim(references, image_id, axis=1, keepdims=False)
        image_keys = chosen[0].reshape(ref_length, head_count, HEAD_DIM)
        image_values = chosen[1].reshape(ref_length, head_count, HEAD_DIM)
        queries = query_frame.reshape(query_frame.shape[0], head_count, HEAD_DIM)
        keys_full = keys_frame.reshape(keys_frame.shape[0], head_count, HEAD_DIM)
        values_full = values_frame.reshape(values_frame.shape[0], head_count, HEAD_DIM)
        result = attend_frame(queries, keys_full, values_full, image_keys, image_values, factor)
        return result.reshape(query_frame.shape[0], feat_width)

    query_moved, pairs_moved = (
        lax.all_to_all(tok_q[None], "rows", split_axis=1, concat_axis=2, tiled=True),
        lax.all_to_all(tok_kv, "rows", split_axis=1, concat_axis=2, tiled=True),
    )
    per_device = frame_count // lax.axis_size("rows")
    local_ids = lax.dynamic_slice_in_dim(ref_ids, lax.axis_index("rows") * per_device, per_device)
    attended = lax.map(spatial_frame, (query_moved[0], pairs_moved[0], pairs_moved[1], local_ids))
    spatial = lax.all_to_all(attended, "rows", split_axis=1, concat_axis=0, tiled=True)
    return (temporal + spatial).astype(jnp.bfloat16)


NEG = -1e30
MESH = pl.DeviceIdType.MESH


def scores_of(keys, queries):
    return lax.dot_general(
        keys, queries, (((1,), (1,)), ((), ())), preferred_element_type=jnp.float32
    )


def kernel(
    n,
    chunks,
    q_hbm,
    kv_hbm,
    ref_hbm,
    ids_ref,
    out_ref,
    qbuf,
    kvbuf,
    rbuf,
    idbuf,
    pref,
    ptime,
    pframe,
    stats,
    vt,
    mine,
    part,
    got,
    local_sem,
    xs_sem,
    xr_sem,
    qs_sem,
    qr_sem,
    is_sem,
    ir_sem,
    ss_sem,
    sr_sem,
    ps_sem,
    pr_sem,
):
    frame_count, row_count, width = q_hbm.shape
    head_count = width // HEAD_DIM
    per_chunk = head_count // chunks
    chunk_width = per_chunk * HEAD_DIM
    tokens = frame_count * row_count
    images, ref_rows = ref_hbm.shape[1], ref_hbm.shape[2]
    span = 2 * ref_rows
    factor = 1.0 / HEAD_DIM**0.5
    me = lax.axis_index("frames")
    has_left, has_right = me >= 1, me <= n - 2
    middle = has_left & has_right
    across = {"rows": 1 - lax.axis_index("rows")}
    ahead = [{"frames": lax.rem(me + d, n)} for d in range(n)]
    right, left = ahead[1], ahead[n - 1]
    banded = (0, 1, n - 1)
    far_slots = list(range(2, n - 1))
    own_rows, far_rows = pl.ds(0, ref_rows), pl.ds(ref_rows, ref_rows)

    loads = [
        pltpu.make_async_copy(q_hbm, qbuf.at[0], local_sem.at[0]),
        pltpu.make_async_copy(ref_hbm.at[0], rbuf.at[0, :, own_rows], local_sem.at[1]),
        pltpu.make_async_copy(kv_hbm, kvbuf.at[0], local_sem.at[2]),
        pltpu.make_async_copy(ref_hbm.at[1], rbuf.at[1, :, own_rows], local_sem.at[3]),
    ]
    for copy in loads:
        copy.start()

    barrier = pltpu.get_barrier_semaphore()
    for d in range(1, n):
        pl.semaphore_signal(barrier, inc=1, device_id=ahead[d], device_id_type=MESH)
    pl.semaphore_signal(barrier, inc=1, device_id=across, device_id_type=MESH)

    lane_frame = lax.broadcasted_iota(jnp.int32, (8, tokens), 1) // row_count
    which = jnp.zeros((8, tokens), jnp.int32)
    for f in range(frame_count):
        which = jnp.where(lane_frame == f, ids_ref[f], which)
    idbuf[0] = which

    pl.semaphore_wait(barrier, n)

    def remote(src, dst, send, recv, where):
        return pltpu.make_async_remote_copy(
            src_ref=src, dst_ref=dst, send_sem=send, recv_sem=recv,
            device_id=where, device_id_type=MESH,
        )

    def part_of(c):
        return pl.ds(c * chunk_width, chunk_width)

    def x_copy(c, k):
        cut = part_of(c)
        if k % 2 == 0:
            src, dst = ref_hbm.at[k // 2, :, :, cut], rbuf.at[k // 2, :, far_rows, cut]
        else:
            src, dst = kv_hbm.at[k // 2, :, :, cut], kvbuf.at[1, k // 2, :, :, cut]
        return remote(src, dst, xs_sem.at[c, k], xr_sem.at[c, k], across)

    def q_right(c, d):
        cut = part_of(c)
        src = q_hbm.at[:, :, cut] if d == 0 else qbuf.at[d, :, :, cut]
        return remote(
            src, qbuf.at[d + 1, :, :, cut], qs_sem.at[c, d], qr_sem.at[c, d + 1], right
        )

    def q_left(c, d):
        cut = part_of(c)
        src = q_hbm.at[:, :, cut] if d == 0 else qbuf.at[d, :, :, cut]
        to = (d if d else n) - 1
        return remote(
            src, qbuf.at[to, :, :, cut], qs_sem.at[c, d if d else n], qr_sem.at[c, to], left
        )

    def q_moves(d):
        if d == 0:
            return [(has_right, q_right), (has_left, q_left)]
        moves = []
        if d < n - 1:
            moves.append(((d <= me) & has_right, q_right))
        if d > 1:
            moves.append(((d > me) & has_left, q_left))
        return moves

    def send_queries(c, d):
        for flag, make in q_moves(d):
            pl.when(flag)(lambda make=make: make(c, d).start())

    def take_queries(c, d):
        cut = part_of(c)
        held = qbuf.at[d, :, :, cut]
        remote(held, held, qs_sem.at[c, d], qr_sem.at[c, d], right).wait_recv()
        send_queries(c, d)

    icopies = [None] + [
        remote(idbuf.at[0], idbuf.at[d], is_sem.at[d], ir_sem.at[d], ahead[d]) for d in range(1, n)
    ]
    for copy in icopies[1:]:
        copy.start()
    for c in range(chunks):
        send_queries(c, 0)
        for k in range(4):
            x_copy(c, k).start()

    row = lax.broadcasted_iota(jnp.int32, (tokens, tokens), 0)
    col = lax.broadcasted_iota(jnp.int32, (tokens, tokens), 1)
    key_frame, key_row = row // row_count, row % row_count
    query_frame, query_row = col // row_count, col % row_count

    def in_band(d):
        mask = key_row == query_row
        if d == 1:
            mask = mask & (key_frame <= query_frame)
        elif d == n - 1:
            mask = mask & (key_frame >= query_frame)
        return mask

    def heads_of(c):
        return [(h, pl.ds(h * HEAD_DIM, HEAD_DIM)) for h in range(c * per_chunk, (c + 1) * per_chunk)]

    def score_block(c, d):
        for h, cut in heads_of(c):
            query = qbuf[d, :, :, cut].reshape(tokens, HEAD_DIM)
            image_keys = rbuf[0, :, :, cut].reshape(images * span, HEAD_DIM)
            both = scores_of(image_keys, query)
            chosen = idbuf[d][0:1]
            score = both[0:span]
            for i in range(1, images):
                score = jnp.where(chosen == i, both[i * span : (i + 1) * span], score)
            score = score * factor
            top = jnp.max(score, axis=0, keepdims=True)
            time_top, time_sum = jnp.zeros_like(top), jnp.zeros_like(top)
            if d in banded:
                keys = kvbuf[0, 0, :, :, cut].reshape(tokens, HEAD_DIM)
                near = scores_of(keys, query) * factor
                time_score = jnp.where(in_band(d), near, NEG)
                time_top = jnp.max(time_score, axis=0, keepdims=True)
                time_exp = jnp.exp(time_score - time_top)
                time_sum = jnp.sum(time_exp, axis=0, keepdims=True)
                ptime[d, h] = time_exp
            if d == 0:
                other_keys = kvbuf[1, 0, :, :, cut].reshape(tokens, HEAD_DIM)
                other = scores_of(other_keys, query) * factor
                near = jnp.where(key_frame == query_frame, near, NEG)
                other = jnp.where(key_frame == query_frame, other, NEG)
                top = jnp.maximum(top, jnp.max(near, axis=0, keepdims=True))
                top = jnp.maximum(top, jnp.max(other, axis=0, keepdims=True))
                near = jnp.exp(near - top)
                other = jnp.exp(other - top)
                pframe[h, 0] = near
                pframe[h, 1] = other
            score = jnp.exp(score - top)
            total = jnp.sum(score, axis=0, keepdims=True)
            if d == 0:
                total = total + jnp.sum(near, axis=0, keepdims=True)
                total = total + jnp.sum(other, axis=0, keepdims=True)
            pref[d, h] = score
            stats[0, c, d, h % per_chunk] = jnp.concatenate(
                [top, total, time_top, time_sum], axis=0
            )

    def scale_of(c, d, h, k):
        tops, sums = [], []
        for e in range(n):
            place = (d - e) % n
            if k == 2 and place not in banded:
                continue
            block = stats[e, c, place, h % per_chunk]
            tops.append(block[k : k + 1])
            sums.append(block[k + 1 : k + 2])
        top = functools.reduce(jnp.maximum, tops)
        total = sum(s * jnp.exp(t - top) for t, s in zip(tops, sums))
        return jnp.exp(tops[0] - top) / total

    def value_block(c, d):
        for h, cut in heads_of(c):
            chosen = idbuf[d][0:1]
            scale = scale_of(c, d, h, 0)
            weight = pref[d, h] * scale
            weights = [
                jnp.where(chosen == i, weight, 0.0).astype(jnp.bfloat16) for i in range(images)
            ]
            if d in banded:
                weights.append((ptime[d, h] * scale_of(c, d, h, 2)).astype(jnp.bfloat16))
            weight = jnp.concatenate(weights, axis=0)
            values = vt[h, :, 0 : weight.shape[0]]
            result = jnp.dot(values, weight, preferred_element_type=jnp.float32)
            if d == 0:
                for i in range(2):
                    start = images * span + i * tokens
                    result = result + jnp.dot(
                        vt[h, :, start : start + tokens],
                        (pframe[h, i] * scale).astype(jnp.bfloat16),
                        preferred_element_type=jnp.float32,
                    )
            mine[d, h] = result

    def turn_values(c):
        for h, cut in heads_of(c):
            blocks = [
                rbuf[1, :, :, cut].reshape(images * span, HEAD_DIM),
                kvbuf[0, 1, :, :, cut].reshape(tokens, HEAD_DIM),
                kvbuf[1, 1, :, :, cut].reshape(tokens, HEAD_DIM),
            ]
            values = jnp.concatenate(blocks, axis=0).astype(jnp.float32)
            vt[h] = values.T.astype(jnp.bfloat16)

    def stats_copy(c, d):
        return remote(stats.at[0, c], stats.at[d, c], ss_sem.at[c, d], sr_sem.at[c, d], ahead[d])

    def p_left(c, d):
        held = pl.ds(c * per_chunk, per_chunk)
        return remote(
            part.at[d, held], got.at[d - 1, held], ps_sem.at[c, d], pr_sem.at[c, d - 1], left
        )

    def p_right(c, d):
        held = pl.ds(c * per_chunk, per_chunk)
        return remote(
            part.at[d, held], got.at[d + 1, held], ps_sem.at[c, d], pr_sem.at[c, d + 1], right
        )

    def p_wait(c, d):
        held = got.at[d, pl.ds(c * per_chunk, per_chunk)]
        remote(held, held, ps_sem.at[c, 0], pr_sem.at[c, d], right).wait_recv()

    def pass_on(c, d, gather):
        heads = [h for h, _ in heads_of(c)]
        if gather:
            p_wait(c, d)
        for h in heads:
            total = mine[d, h]
            if gather:
                total = total + got[d, h].astype(jnp.float32)
            part[d, h] = total.astype(jnp.bfloat16)
        pl.when(d <= me)(lambda: p_left(c, d).start())
        pl.when(d > me)(lambda: p_right(c, d).start())

    chain = far_slots + [n - 1, 1]

    def scores(c):
        for d in [0, 1, n - 1] + far_slots:
            if d == 0:
                x_copy(c, 0).wait_recv()
                x_copy(c, 1).wait_recv()
            score_block(c, d)
            if c + 1 < chunks:
                if d == 0:
                    take_queries(c + 1, 1)
                    take_queries(c + 1, n - 1)
                elif d == 1:
                    for far in far_slots:
                        take_queries(c + 1, far)
        for d in range(1, n):
            stats_copy(c, d).start()

    def values(c):
        x_copy(c, 2).wait_recv()
        x_copy(c, 3).wait_recv()
        turn_values(c)
        for d in range(1, n):
            stats_copy(c, d).wait_recv()
        for d in chain:
            value_block(c, d)

        @pl.when(jnp.logical_not(middle))
        def _():
            for d in chain:
                pass_on(c, d, False)

        value_block(c, 0)

    def combine(c):
        @pl.when(middle)
        def _():
            for d in chain:
                pass_on(c, d, True)

    def finish(c):
        pl.when(has_right)(lambda: p_wait(c, 0))
        pl.when(has_left)(lambda: p_wait(c, n))
        for h, cut in heads_of(c):
            total = mine[0, h]
            total = total + jnp.where(has_right, got[0, h].astype(jnp.float32), 0.0)
            total = total + jnp.where(has_left, got[n, h].astype(jnp.float32), 0.0)
            out_ref[:, :, cut] = total.T.reshape(frame_count, row_count, HEAD_DIM).astype(
                jnp.bfloat16
            )

    got[0] = jnp.zeros_like(got[0])
    got[n] = jnp.zeros_like(got[n])
    for copy in loads:
        copy.wait()
    for d in range(1, n):
        icopies[d].wait_recv()
    take_queries(0, 1)
    take_queries(0, n - 1)
    for d in far_slots:
        take_queries(0, d)
    scores(0)
    for c in range(chunks):
        if c + 1 < chunks:
            scores(c + 1)
        if c >= 1:
            combine(c - 1)
        values(c)
    combine(chunks - 1)
    for c in range(chunks):
        finish(c)

    for copy in icopies[1:]:
        copy.wait_send()
    for c in range(chunks):
        for k in range(4):
            x_copy(c, k).wait_send()
        for d in range(n):
            for flag, make in q_moves(d):
                pl.when(flag)(lambda make=make: make(c, d).wait_send())
        for d in range(1, n):
            stats_copy(c, d).wait_send()
            held = part.at[d, pl.ds(c * per_chunk, per_chunk)]
            remote(held, held, ps_sem.at[c, d], pr_sem.at[c, d], right).wait_send()


def local_kernel(tok_q, tok_kv, ref_kv, ref_ids):
    n = lax.axis_size("frames")
    frame_count, row_count, width = tok_q.shape
    heads = width // HEAD_DIM
    chunks = heads // 2
    tokens = frame_count * row_count
    images, ref_rows = ref_kv.shape[1:3]
    span = 2 * ref_rows
    dma = pltpu.SemaphoreType.DMA
    in_hbm = pl.BlockSpec(memory_space=pltpu.HBM)
    return pl.pallas_call(
        functools.partial(kernel, n, chunks),
        out_shape=jax.ShapeDtypeStruct(tok_q.shape, jnp.bfloat16),
        in_specs=[in_hbm] * 3 + [pl.BlockSpec(memory_space=pltpu.SMEM)],
        out_specs=pl.BlockSpec(memory_space=pltpu.VMEM),
        scratch_shapes=[
            pltpu.VMEM((n,) + tok_q.shape, jnp.bfloat16),
            pltpu.VMEM((2,) + tok_kv.shape, jnp.bfloat16),
            pltpu.VMEM((2, images, span, width), jnp.bfloat16),
            pltpu.VMEM((n, 8, tokens), jnp.int32),
            pltpu.VMEM((n, heads, span, tokens), jnp.float32),
            pltpu.VMEM((n, heads, tokens, tokens), jnp.float32),
            pltpu.VMEM((heads, 2, tokens, tokens), jnp.float32),
            pltpu.VMEM((n, chunks, n, heads // chunks, 4, tokens), jnp.float32),
            pltpu.VMEM((heads, HEAD_DIM, images * span + 2 * tokens), jnp.bfloat16),
            pltpu.VMEM((n, heads, HEAD_DIM, tokens), jnp.float32),
            pltpu.VMEM((n, heads, HEAD_DIM, tokens), jnp.bfloat16),
            pltpu.VMEM((n + 1, heads, HEAD_DIM, tokens), jnp.bfloat16),
            dma((4,)),
            dma((chunks, 4)),
            dma((chunks, 4)),
            dma((chunks, n + 1)),
            dma((chunks, n)),
            dma((n,)),
            dma((n,)),
            dma((chunks, n)),
            dma((chunks, n)),
            dma((chunks, n)),
            dma((chunks, n + 1)),
        ],
        compiler_params=pltpu.CompilerParams(
            collective_id=0, has_side_effects=True, vmem_limit_bytes=64 * 1024 * 1024
        ),
    )(tok_q, tok_kv, ref_kv, ref_ids)


def local(tok_q, tok_kv, ref_kv, ref_ids):
    frame_count, row_count, width = tok_q.shape
    fits = (
        3 <= lax.axis_size("frames") <= 4
        and lax.axis_size("rows") == 2
        and frame_count == BAND
        and row_count % 16 == 0
        and frame_count * row_count == 128
        and ref_kv.shape[2] % 16 == 0
        and (width // HEAD_DIM) % 2 == 0
    )
    return (local_kernel if fits else local_general)(tok_q, tok_kv, ref_kv, ref_ids)


def solution(mesh):
    placed = (
        P(("clip", "frames"), "rows", "heads"),
        P(None, ("clip", "frames"), "rows", "heads"),
        P(None, "clip", ("frames", "rows"), "heads"),
        P(("clip", "frames")),
    )
    return jax.shard_map(
        local,
        mesh=mesh,
        in_specs=placed,
        out_specs=P(("clip", "frames"), "rows", "heads"),
        check_vma=False,
    )
```

```python
import functools

import jax
import jax.numpy as jnp
from jax import lax
from jax.experimental import pallas as pl
from jax.experimental.pallas import tpu as pltpu
from jax.sharding import PartitionSpec as P

HEAD_DIM = 128
BAND = 8


def padded_2(value, sides, width):
    for axis, dim in sides:
        devices, length = (lax.axis_size(axis), value.shape[dim])
        up = [(i, (i + 1) % devices) for i in range(devices)]
        down = [(j, i) for i, j in up]
        last = lax.slice_in_dim(value, length - width, length, axis=dim)
        first = lax.slice_in_dim(value, 0, width, axis=dim)
        before = lax.ppermute(last, axis, up)
        after = lax.ppermute(first, axis, down)
        value = jnp.concatenate([before, value, after], axis=dim)
    return value


def attend_frame(query, frame_keys, frame_values, image_keys, image_values, factor):
    local_scores = (
        jnp.einsum("thd,shd->hts", query, frame_keys, preferred_element_type=jnp.float32) * factor
    )
    image_scores = (
        jnp.einsum("thd,shd->hts", query, image_keys, preferred_element_type=jnp.float32) * factor
    )
    top = jnp.maximum(jnp.max(local_scores, axis=-1), jnp.max(image_scores, axis=-1))
    local_exp = jnp.exp(local_scores - top[..., None])
    image_exp = jnp.exp(image_scores - top[..., None])
    total = jnp.sum(local_exp, axis=-1) + jnp.sum(image_exp, axis=-1)
    local_weights = (local_exp / total[..., None]).astype(jnp.bfloat16)
    image_weights = (image_exp / total[..., None]).astype(jnp.bfloat16)
    result = jnp.einsum(
        "hts,shd->thd", local_weights, frame_values, preferred_element_type=jnp.float32
    )
    result = result + jnp.einsum(
        "hts,shd->thd", image_weights, image_values, preferred_element_type=jnp.float32
    )
    return result


def local_general(tok_q, tok_kv, ref_kv, ref_ids):
    frame_count, row_count, feat_width = tok_q.shape
    head_count = feat_width // HEAD_DIM
    factor = 1.0 / HEAD_DIM**0.5
    query_heads = tok_q.reshape(frame_count, row_count, head_count, HEAD_DIM)
    padded = padded_2(tok_kv, (("frames", 1),), BAND)
    band_scores = []
    for offset in range(2 * BAND + 1):
        key_block = padded[0, offset : offset + frame_count].reshape(
            frame_count, row_count, head_count, HEAD_DIM
        )
        band_scores.append(
            jnp.einsum("frhd,frhd->frh", query_heads, key_block, preferred_element_type=jnp.float32)
            * factor
        )
    band_weights = jax.nn.softmax(jnp.stack(band_scores), axis=0).astype(jnp.bfloat16)
    temporal = jnp.zeros((frame_count, row_count, head_count, HEAD_DIM), jnp.float32)
    for offset in range(2 * BAND + 1):
        value_block = padded[1, offset : offset + frame_count].reshape(
            frame_count, row_count, head_count, HEAD_DIM
        )
        temporal = temporal + jnp.einsum(
            "frh,frhd->frhd", band_weights[offset], value_block, preferred_element_type=jnp.float32
        )
    temporal = temporal.reshape(frame_count, row_count, feat_width)
    references = lax.all_gather(ref_kv, ("frames", "rows"), axis=2, tiled=True)
    ref_length = references.shape[2]

    def spatial_frame(inputs):
        query_frame, keys_frame, values_frame, image_id = inputs
        chosen = lax.dynamic_index_in_dim(references, image_id, axis=1, keepdims=False)
        image_keys = chosen[0].reshape(ref_length, head_count, HEAD_DIM)
        image_values = chosen[1].reshape(ref_length, head_count, HEAD_DIM)
        queries = query_frame.reshape(query_frame.shape[0], head_count, HEAD_DIM)
        keys_full = keys_frame.reshape(keys_frame.shape[0], head_count, HEAD_DIM)
        values_full = values_frame.reshape(values_frame.shape[0], head_count, HEAD_DIM)
        result = attend_frame(queries, keys_full, values_full, image_keys, image_values, factor)
        return result.reshape(query_frame.shape[0], feat_width)

    query_moved, pairs_moved = (
        lax.all_to_all(tok_q[None], "rows", split_axis=1, concat_axis=2, tiled=True),
        lax.all_to_all(tok_kv, "rows", split_axis=1, concat_axis=2, tiled=True),
    )
    per_device = frame_count // lax.axis_size("rows")
    local_ids = lax.dynamic_slice_in_dim(ref_ids, lax.axis_index("rows") * per_device, per_device)
    attended = lax.map(spatial_frame, (query_moved[0], pairs_moved[0], pairs_moved[1], local_ids))
    spatial = lax.all_to_all(attended, "rows", split_axis=1, concat_axis=0, tiled=True)
    return (temporal + spatial).astype(jnp.bfloat16)


NEG = -1e30
MESH = pl.DeviceIdType.MESH


def scores_of(keys, queries):
    return lax.dot_general(
        keys, queries, (((1,), (1,)), ((), ())), preferred_element_type=jnp.float32
    )


def kernel(
    n,
    chunks,
    q_hbm,
    kv_hbm,
    ref_hbm,
    ids_ref,
    out_ref,
    qbuf,
    kvbuf,
    rbuf,
    idbuf,
    pref,
    ptime,
    pframe,
    stats,
    vt,
    mine,
    part,
    got,
    local_sem,
    xs_sem,
    xr_sem,
    qs_sem,
    qr_sem,
    is_sem,
    ir_sem,
    ss_sem,
    sr_sem,
    ps_sem,
    pr_sem,
):
    frame_count, row_count, width = q_hbm.shape
    head_count = width // HEAD_DIM
    per_chunk = head_count // chunks
    chunk_width = per_chunk * HEAD_DIM
    tokens = frame_count * row_count
    images, ref_rows = ref_hbm.shape[1], ref_hbm.shape[2]
    span = 2 * ref_rows
    factor = 1.0 / HEAD_DIM**0.5
    me = lax.axis_index("frames")
    has_left, has_right = me >= 1, me <= n - 2
    middle = has_left & has_right
    across = {"rows": 1 - lax.axis_index("rows")}
    ahead = [{"frames": lax.rem(me + d, n)} for d in range(n)]
    right, left = ahead[1], ahead[n - 1]
    banded = (0, 1, n - 1)
    far_slots = list(range(2, n - 1))
    own_rows, far_rows = pl.ds(0, ref_rows), pl.ds(ref_rows, ref_rows)

    loads = [
        pltpu.make_async_copy(q_hbm, qbuf.at[0], local_sem.at[0]),
        pltpu.make_async_copy(ref_hbm.at[0], rbuf.at[0, :, own_rows], local_sem.at[1]),
        pltpu.make_async_copy(kv_hbm, kvbuf.at[0], local_sem.at[2]),
        pltpu.make_async_copy(ref_hbm.at[1], rbuf.at[1, :, own_rows], local_sem.at[3]),
    ]
    for copy in loads:
        copy.start()

    barrier = pltpu.get_barrier_semaphore()
    for d in range(1, n):
        pl.semaphore_signal(barrier, inc=1, device_id=ahead[d], device_id_type=MESH)
    pl.semaphore_signal(barrier, inc=1, device_id=across, device_id_type=MESH)

    lane_frame = lax.broadcasted_iota(jnp.int32, (8, tokens), 1) // row_count
    which = jnp.zeros((8, tokens), jnp.int32)
    for f in range(frame_count):
        which = jnp.where(lane_frame == f, ids_ref[f], which)
    idbuf[0] = which

    pl.semaphore_wait(barrier, n)

    def remote(src, dst, send, recv, where):
        return pltpu.make_async_remote_copy(
            src_ref=src, dst_ref=dst, send_sem=send, recv_sem=recv,
            device_id=where, device_id_type=MESH,
        )

    def part_of(c):
        return pl.ds(c * chunk_width, chunk_width)

    def x_copy(c, k):
        cut = part_of(c)
        if k % 2 == 0:
            src, dst = ref_hbm.at[k // 2, :, :, cut], rbuf.at[k // 2, :, far_rows, cut]
        else:
            src, dst = kv_hbm.at[k // 2, :, :, cut], kvbuf.at[1, k // 2, :, :, cut]
        return remote(src, dst, xs_sem.at[c, k], xr_sem.at[c, k], across)

    def q_right(c, d):
        cut = part_of(c)
        src = q_hbm.at[:, :, cut] if d == 0 else qbuf.at[d, :, :, cut]
        return remote(
            src, qbuf.at[d + 1, :, :, cut], qs_sem.at[c, d], qr_sem.at[c, d + 1], right
        )

    def q_left(c, d):
        cut = part_of(c)
        src = q_hbm.at[:, :, cut] if d == 0 else qbuf.at[d, :, :, cut]
        to = (d if d else n) - 1
        return remote(
            src, qbuf.at[to, :, :, cut], qs_sem.at[c, d if d else n], qr_sem.at[c, to], left
        )

    def q_moves(d):
        if d == 0:
            return [(has_right, q_right), (has_left, q_left)]
        moves = []
        if d < n - 1:
            moves.append(((d <= me) & has_right, q_right))
        if d > 1:
            moves.append(((d > me) & has_left, q_left))
        return moves

    def send_queries(c, d):
        for flag, make in q_moves(d):
            pl.when(flag)(lambda make=make: make(c, d).start())

    def take_queries(c, d):
        cut = part_of(c)
        held = qbuf.at[d, :, :, cut]
        remote(held, held, qs_sem.at[c, d], qr_sem.at[c, d], right).wait_recv()
        send_queries(c, d)

    icopies = [None] + [
        remote(idbuf.at[0], idbuf.at[d], is_sem.at[d], ir_sem.at[d], ahead[d]) for d in range(1, n)
    ]
    for copy in icopies[1:]:
        copy.start()
    for c in range(chunks):
        send_queries(c, 0)
        for k in range(4):
            x_copy(c, k).start()

    slots = [n - 1, 0, 1] + far_slots
    banded_width, all_width = 3 * tokens, n * tokens
    here = slice(tokens, 2 * tokens)

    def grid(width, axis):
        return lax.broadcasted_iota(jnp.int32, (frame_count, row_count, width), axis)

    def same_row(width):
        return grid(width, 1) == grid(width, 2) % row_count

    def same_frame():
        return grid(tokens, 0) == grid(tokens, 2) // row_count

    def in_band():
        keys = lax.broadcasted_iota(jnp.int32, (frame_count, banded_width), 0)
        lane = lax.broadcasted_iota(jnp.int32, (frame_count, banded_width), 1)
        block, frame = lane // tokens, lane % tokens // row_count
        return (
            ((block == 0) & (keys >= frame)) | (block == 1) | ((block == 2) & (keys <= frame))
        )

    def heads_of(c):
        return [(h, pl.ds(h * HEAD_DIM, HEAD_DIM)) for h in range(c * per_chunk, (c + 1) * per_chunk)]

    def side_by_side(rows):
        return jnp.concatenate(rows, axis=1)

    def score_block(c):
        chosen = side_by_side([idbuf[d][0:1] for d in slots])
        for h, cut in heads_of(c):
            query = jnp.concatenate(
                [qbuf[d, :, :, cut].reshape(tokens, HEAD_DIM) for d in slots], axis=0
            )
            image_keys = rbuf[0, :, :, cut].reshape(images * span, HEAD_DIM)
            both = scores_of(image_keys, query)
            score = both[0:span]
            for i in range(1, images):
                score = jnp.where(chosen == i, both[i * span : (i + 1) * span], score)
            score = score * factor
            keys = kvbuf[0, 0, :, :, cut].reshape(tokens, HEAD_DIM)
            near = scores_of(keys, query[0:banded_width]) * factor
            near = near.reshape(frame_count, row_count, banded_width)
            time = jnp.sum(jnp.where(same_row(banded_width), near, 0.0), axis=1)
            time = jnp.where(in_band(), time, NEG)
            time_top = jnp.max(time, axis=0, keepdims=True)
            time = jnp.exp(time - time_top)
            ptime[h] = time
            time_sum = jnp.sum(time, axis=0, keepdims=True)
            other_keys = kvbuf[1, 0, :, :, cut].reshape(tokens, HEAD_DIM)
            other = scores_of(other_keys, query[here]) * factor
            other = other.reshape(frame_count, row_count, tokens)
            frame = jnp.concatenate(
                [
                    jnp.sum(jnp.where(same_frame(), near[:, :, here], 0.0), axis=0),
                    jnp.sum(jnp.where(same_frame(), other, 0.0), axis=0),
                ],
                axis=0,
            )
            top = jnp.max(score, axis=0, keepdims=True)
            frame_top = jnp.max(frame, axis=0, keepdims=True)
            top = side_by_side(
                [
                    top[:, 0:tokens],
                    jnp.maximum(top[:, here], frame_top),
                    top[:, 2 * tokens :],
                ]
            )
            frame = jnp.exp(frame - top[:, here])
            pframe[h] = frame
            frame_sum = jnp.sum(frame, axis=0, keepdims=True)
            score = jnp.exp(score - top)
            pref[h] = score
            total = jnp.sum(score, axis=0, keepdims=True)
            for i, d in enumerate(slots):
                at = slice(i * tokens, (i + 1) * tokens)
                rows = [top[:, at], total[:, at] + frame_sum if d == 0 else total[:, at]]
                if d in banded:
                    rows += [time_top[:, at], time_sum[:, at]]
                else:
                    rows += [jnp.zeros((2, tokens), jnp.float32)]
                stats[0, c, d, h % per_chunk] = jnp.concatenate(rows, axis=0)

    def scale_of(c, d, h, k):
        tops, sums = [], []
        for e in range(n):
            place = (d - e) % n
            if k == 2 and place not in banded:
                continue
            block = stats[e, c, place, h % per_chunk]
            tops.append(block[k : k + 1])
            sums.append(block[k + 1 : k + 2])
        top = functools.reduce(jnp.maximum, tops)
        total = sum(s * jnp.exp(t - top) for t, s in zip(tops, sums))
        return jnp.exp(tops[0] - top) / total

    def value_block(c):
        chosen = side_by_side([idbuf[d][0:1] for d in slots])
        for h, cut in heads_of(c):
            scale = side_by_side([scale_of(c, d, h, 0) for d in slots])
            weight = pref[h] * scale
            weight = jnp.concatenate(
                [jnp.where(chosen == i, weight, 0.0).astype(jnp.bfloat16) for i in range(images)],
                axis=0,
            )
            start = images * span
            result = jnp.dot(vt[h, :, 0:start], weight, preferred_element_type=jnp.float32)
            time = ptime[h] * side_by_side([scale_of(c, d, h, 2) for d in slots[:3]])
            time = jnp.where(same_row(banded_width), time[:, None, :], 0.0)
            time = time.reshape(tokens, banded_width).astype(jnp.bfloat16)
            timed = jnp.dot(
                vt[h, :, start : start + tokens], time, preferred_element_type=jnp.float32
            )
            frame = pframe[h] * scale[:, here]
            frames = [
                jnp.where(same_frame(), frame[i * row_count : (i + 1) * row_count][None], 0.0)
                .reshape(tokens, tokens)
                .astype(jnp.bfloat16)
                for i in range(2)
            ]
            framed = jnp.dot(
                vt[h, :, start : start + 2 * tokens],
                jnp.concatenate(frames, axis=0),
                preferred_element_type=jnp.float32,
            )
            for i, d in enumerate(slots):
                at = slice(i * tokens, (i + 1) * tokens)
                piece = result[:, at]
                if d in banded:
                    piece = piece + timed[:, at]
                if d == 0:
                    piece = piece + framed
                mine[d, h] = piece

    def turn_values(c):
        for h, cut in heads_of(c):
            blocks = [
                rbuf[1, :, :, cut].reshape(images * span, HEAD_DIM),
                kvbuf[0, 1, :, :, cut].reshape(tokens, HEAD_DIM),
                kvbuf[1, 1, :, :, cut].reshape(tokens, HEAD_DIM),
            ]
            values = jnp.concatenate(blocks, axis=0).astype(jnp.float32)
            vt[h] = values.T.astype(jnp.bfloat16)

    def stats_copy(c, d):
        return remote(stats.at[0, c], stats.at[d, c], ss_sem.at[c, d], sr_sem.at[c, d], ahead[d])

    def p_left(c, d):
        held = pl.ds(c * per_chunk, per_chunk)
        return remote(
            part.at[d, held], got.at[d - 1, held], ps_sem.at[c, d], pr_sem.at[c, d - 1], left
        )

    def p_right(c, d):
        held = pl.ds(c * per_chunk, per_chunk)
        return remote(
            part.at[d, held], got.at[d + 1, held], ps_sem.at[c, d], pr_sem.at[c, d + 1], right
        )

    def p_wait(c, d):
        held = got.at[d, pl.ds(c * per_chunk, per_chunk)]
        remote(held, held, ps_sem.at[c, 0], pr_sem.at[c, d], right).wait_recv()

    def pass_on(c, d, gather):
        heads = [h for h, _ in heads_of(c)]
        if gather:
            p_wait(c, d)
        for h in heads:
            total = mine[d, h]
            if gather:
                total = total + got[d, h].astype(jnp.float32)
            part[d, h] = total.astype(jnp.bfloat16)
        pl.when(d <= me)(lambda: p_left(c, d).start())
        pl.when(d > me)(lambda: p_right(c, d).start())

    chain = far_slots + [n - 1, 1]

    def scores(c):
        for d in [1, n - 1] + far_slots:
            take_queries(c, d)
        x_copy(c, 0).wait_recv()
        x_copy(c, 1).wait_recv()
        score_block(c)
        for d in range(1, n):
            stats_copy(c, d).start()

    def values(c):
        x_copy(c, 2).wait_recv()
        x_copy(c, 3).wait_recv()
        turn_values(c)
        for d in range(1, n):
            stats_copy(c, d).wait_recv()
        value_block(c)

        @pl.when(jnp.logical_not(middle))
        def _():
            for d in chain:
                pass_on(c, d, False)

    def combine(c):
        @pl.when(middle)
        def _():
            for d in chain:
                pass_on(c, d, True)

    def finish(c):
        pl.when(has_right)(lambda: p_wait(c, 0))
        pl.when(has_left)(lambda: p_wait(c, n))
        for h, cut in heads_of(c):
            total = mine[0, h]
            total = total + jnp.where(has_right, got[0, h].astype(jnp.float32), 0.0)
            total = total + jnp.where(has_left, got[n, h].astype(jnp.float32), 0.0)
            out_ref[:, :, cut] = total.T.reshape(frame_count, row_count, HEAD_DIM).astype(
                jnp.bfloat16
            )

    got[0] = jnp.zeros_like(got[0])
    got[n] = jnp.zeros_like(got[n])
    for copy in loads:
        copy.wait()
    for d in range(1, n):
        icopies[d].wait_recv()
    scores(0)
    for c in range(chunks):
        if c + 1 < chunks:
            scores(c + 1)
        if c >= 1:
            combine(c - 1)
        values(c)
    combine(chunks - 1)
    for c in range(chunks):
        finish(c)

    for copy in icopies[1:]:
        copy.wait_send()
    for c in range(chunks):
        for k in range(4):
            x_copy(c, k).wait_send()
        for d in range(n):
            for flag, make in q_moves(d):
                pl.when(flag)(lambda make=make: make(c, d).wait_send())
        for d in range(1, n):
            stats_copy(c, d).wait_send()
            held = part.at[d, pl.ds(c * per_chunk, per_chunk)]
            remote(held, held, ps_sem.at[c, d], pr_sem.at[c, d], right).wait_send()


def local_kernel(tok_q, tok_kv, ref_kv, ref_ids):
    n = lax.axis_size("frames")
    frame_count, row_count, width = tok_q.shape
    heads = width // HEAD_DIM
    chunks = heads // 2
    tokens = frame_count * row_count
    images, ref_rows = ref_kv.shape[1:3]
    span = 2 * ref_rows
    dma = pltpu.SemaphoreType.DMA
    in_hbm = pl.BlockSpec(memory_space=pltpu.HBM)
    return pl.pallas_call(
        functools.partial(kernel, n, chunks),
        out_shape=jax.ShapeDtypeStruct(tok_q.shape, jnp.bfloat16),
        in_specs=[in_hbm] * 3 + [pl.BlockSpec(memory_space=pltpu.SMEM)],
        out_specs=pl.BlockSpec(memory_space=pltpu.VMEM),
        scratch_shapes=[
            pltpu.VMEM((n,) + tok_q.shape, jnp.bfloat16),
            pltpu.VMEM((2,) + tok_kv.shape, jnp.bfloat16),
            pltpu.VMEM((2, images, span, width), jnp.bfloat16),
            pltpu.VMEM((n, 8, tokens), jnp.int32),
            pltpu.VMEM((heads, span, n * tokens), jnp.float32),
            pltpu.VMEM((heads, frame_count, 3 * tokens), jnp.float32),
            pltpu.VMEM((heads, 2 * row_count, tokens), jnp.float32),
            pltpu.VMEM((n, chunks, n, heads // chunks, 4, tokens), jnp.float32),
            pltpu.VMEM((heads, HEAD_DIM, images * span + 2 * tokens), jnp.bfloat16),
            pltpu.VMEM((n, heads, HEAD_DIM, tokens), jnp.float32),
            pltpu.VMEM((n, heads, HEAD_DIM, tokens), jnp.bfloat16),
            pltpu.VMEM((n + 1, heads, HEAD_DIM, tokens), jnp.bfloat16),
            dma((4,)),
            dma((chunks, 4)),
            dma((chunks, 4)),
            dma((chunks, n + 1)),
            dma((chunks, n)),
            dma((n,)),
            dma((n,)),
            dma((chunks, n)),
            dma((chunks, n)),
            dma((chunks, n)),
            dma((chunks, n + 1)),
        ],
        compiler_params=pltpu.CompilerParams(
            collective_id=0, has_side_effects=True, vmem_limit_bytes=64 * 1024 * 1024
        ),
    )(tok_q, tok_kv, ref_kv, ref_ids)


def local(tok_q, tok_kv, ref_kv, ref_ids):
    frame_count, row_count, width = tok_q.shape
    fits = (
        3 <= lax.axis_size("frames") <= 4
        and lax.axis_size("rows") == 2
        and frame_count == BAND
        and row_count % 16 == 0
        and frame_count * row_count == 128
        and ref_kv.shape[2] % 16 == 0
        and (width // HEAD_DIM) % 2 == 0
    )
    return (local_kernel if fits else local_general)(tok_q, tok_kv, ref_kv, ref_ids)


def solution(mesh):
    placed = (
        P(("clip", "frames"), "rows", "heads"),
        P(None, ("clip", "frames"), "rows", "heads"),
        P(None, "clip", ("frames", "rows"), "heads"),
        P(("clip", "frames")),
    )
    return jax.shard_map(
        local,
        mesh=mesh,
        in_specs=placed,
        out_specs=P(("clip", "frames"), "rows", "heads"),
        check_vma=False,
    )
```

```python
import functools

import jax
import jax.numpy as jnp
from jax import lax
from jax.experimental import pallas as pl
from jax.experimental.pallas import tpu as pltpu
from jax.sharding import PartitionSpec as P

HEAD_DIM = 128
BAND = 8


def padded_2(value, sides, width):
    for axis, dim in sides:
        devices, length = (lax.axis_size(axis), value.shape[dim])
        up = [(i, (i + 1) % devices) for i in range(devices)]
        down = [(j, i) for i, j in up]
        last = lax.slice_in_dim(value, length - width, length, axis=dim)
        first = lax.slice_in_dim(value, 0, width, axis=dim)
        before = lax.ppermute(last, axis, up)
        after = lax.ppermute(first, axis, down)
        value = jnp.concatenate([before, value, after], axis=dim)
    return value


def attend_frame(query, frame_keys, frame_values, image_keys, image_values, factor):
    local_scores = (
        jnp.einsum("thd,shd->hts", query, frame_keys, preferred_element_type=jnp.float32) * factor
    )
    image_scores = (
        jnp.einsum("thd,shd->hts", query, image_keys, preferred_element_type=jnp.float32) * factor
    )
    top = jnp.maximum(jnp.max(local_scores, axis=-1), jnp.max(image_scores, axis=-1))
    local_exp = jnp.exp(local_scores - top[..., None])
    image_exp = jnp.exp(image_scores - top[..., None])
    total = jnp.sum(local_exp, axis=-1) + jnp.sum(image_exp, axis=-1)
    local_weights = (local_exp / total[..., None]).astype(jnp.bfloat16)
    image_weights = (image_exp / total[..., None]).astype(jnp.bfloat16)
    result = jnp.einsum(
        "hts,shd->thd", local_weights, frame_values, preferred_element_type=jnp.float32
    )
    result = result + jnp.einsum(
        "hts,shd->thd", image_weights, image_values, preferred_element_type=jnp.float32
    )
    return result


def local_general(tok_q, tok_kv, ref_kv, ref_ids):
    frame_count, row_count, feat_width = tok_q.shape
    head_count = feat_width // HEAD_DIM
    factor = 1.0 / HEAD_DIM**0.5
    query_heads = tok_q.reshape(frame_count, row_count, head_count, HEAD_DIM)
    padded = padded_2(tok_kv, (("frames", 1),), BAND)
    band_scores = []
    for offset in range(2 * BAND + 1):
        key_block = padded[0, offset : offset + frame_count].reshape(
            frame_count, row_count, head_count, HEAD_DIM
        )
        band_scores.append(
            jnp.einsum("frhd,frhd->frh", query_heads, key_block, preferred_element_type=jnp.float32)
            * factor
        )
    band_weights = jax.nn.softmax(jnp.stack(band_scores), axis=0).astype(jnp.bfloat16)
    temporal = jnp.zeros((frame_count, row_count, head_count, HEAD_DIM), jnp.float32)
    for offset in range(2 * BAND + 1):
        value_block = padded[1, offset : offset + frame_count].reshape(
            frame_count, row_count, head_count, HEAD_DIM
        )
        temporal = temporal + jnp.einsum(
            "frh,frhd->frhd", band_weights[offset], value_block, preferred_element_type=jnp.float32
        )
    temporal = temporal.reshape(frame_count, row_count, feat_width)
    references = lax.all_gather(ref_kv, ("frames", "rows"), axis=2, tiled=True)
    ref_length = references.shape[2]

    def spatial_frame(inputs):
        query_frame, keys_frame, values_frame, image_id = inputs
        chosen = lax.dynamic_index_in_dim(references, image_id, axis=1, keepdims=False)
        image_keys = chosen[0].reshape(ref_length, head_count, HEAD_DIM)
        image_values = chosen[1].reshape(ref_length, head_count, HEAD_DIM)
        queries = query_frame.reshape(query_frame.shape[0], head_count, HEAD_DIM)
        keys_full = keys_frame.reshape(keys_frame.shape[0], head_count, HEAD_DIM)
        values_full = values_frame.reshape(values_frame.shape[0], head_count, HEAD_DIM)
        result = attend_frame(queries, keys_full, values_full, image_keys, image_values, factor)
        return result.reshape(query_frame.shape[0], feat_width)

    query_moved, pairs_moved = (
        lax.all_to_all(tok_q[None], "rows", split_axis=1, concat_axis=2, tiled=True),
        lax.all_to_all(tok_kv, "rows", split_axis=1, concat_axis=2, tiled=True),
    )
    per_device = frame_count // lax.axis_size("rows")
    local_ids = lax.dynamic_slice_in_dim(ref_ids, lax.axis_index("rows") * per_device, per_device)
    attended = lax.map(spatial_frame, (query_moved[0], pairs_moved[0], pairs_moved[1], local_ids))
    spatial = lax.all_to_all(attended, "rows", split_axis=1, concat_axis=0, tiled=True)
    return (temporal + spatial).astype(jnp.bfloat16)


NEG = -1e30
MESH = pl.DeviceIdType.MESH


def scores_of(keys, queries):
    return lax.dot_general(
        keys, queries, (((1,), (1,)), ((), ())), preferred_element_type=jnp.float32
    )


def kernel(
    n,
    chunks,
    q_hbm,
    kv_hbm,
    ref_hbm,
    ids_ref,
    out_ref,
    qbuf,
    kvbuf,
    rbuf,
    idbuf,
    pref,
    ptime,
    pframe,
    stats,
    vt,
    mine,
    part,
    got,
    local_sem,
    xs_sem,
    xr_sem,
    qs_sem,
    qr_sem,
    is_sem,
    ir_sem,
    ss_sem,
    sr_sem,
    ps_sem,
    pr_sem,
):
    frame_count, row_count, width = q_hbm.shape
    head_count = width // HEAD_DIM
    per_chunk = head_count // chunks
    chunk_width = per_chunk * HEAD_DIM
    tokens = frame_count * row_count
    images, ref_rows = ref_hbm.shape[1], ref_hbm.shape[2]
    span = 2 * ref_rows
    factor = 1.0 / HEAD_DIM**0.5
    me = lax.axis_index("frames")
    has_left, has_right = me >= 1, me <= n - 2
    middle = has_left & has_right
    across = {"rows": 1 - lax.axis_index("rows")}
    ahead = [{"frames": lax.rem(me + d, n)} for d in range(n)]
    right, left = ahead[1], ahead[n - 1]
    banded = (0, 1, n - 1)
    far_slots = list(range(2, n - 1))
    own_rows, far_rows = pl.ds(0, ref_rows), pl.ds(ref_rows, ref_rows)

    loads = [
        pltpu.make_async_copy(q_hbm, qbuf.at[0], local_sem.at[0]),
        pltpu.make_async_copy(ref_hbm.at[0], rbuf.at[0, :, own_rows], local_sem.at[1]),
        pltpu.make_async_copy(kv_hbm, kvbuf.at[0], local_sem.at[2]),
        pltpu.make_async_copy(ref_hbm.at[1], rbuf.at[1, :, own_rows], local_sem.at[3]),
    ]
    for copy in loads:
        copy.start()

    barrier = pltpu.get_barrier_semaphore()
    for d in range(1, n):
        pl.semaphore_signal(barrier, inc=1, device_id=ahead[d], device_id_type=MESH)
    pl.semaphore_signal(barrier, inc=1, device_id=across, device_id_type=MESH)

    lane_frame = lax.broadcasted_iota(jnp.int32, (8, tokens), 1) // row_count
    which = jnp.zeros((8, tokens), jnp.int32)
    for f in range(frame_count):
        which = jnp.where(lane_frame == f, ids_ref[f], which)
    idbuf[0] = which

    pl.semaphore_wait(barrier, n)

    def remote(src, dst, send, recv, where):
        return pltpu.make_async_remote_copy(
            src_ref=src, dst_ref=dst, send_sem=send, recv_sem=recv,
            device_id=where, device_id_type=MESH,
        )

    def part_of(c):
        return pl.ds(c * chunk_width, chunk_width)

    def x_copy(c, k):
        cut = part_of(c)
        if k % 2 == 0:
            src, dst = ref_hbm.at[k // 2, :, :, cut], rbuf.at[k // 2, :, far_rows, cut]
        else:
            src, dst = kv_hbm.at[k // 2, :, :, cut], kvbuf.at[1, k // 2, :, :, cut]
        return remote(src, dst, xs_sem.at[c, k], xr_sem.at[c, k], across)

    def x_keys(c):
        if c < chunks:
            x_copy(c, 0).start()
            x_copy(c, 1).start()

    def x_values(c):
        if c < chunks:
            x_copy(c, 2).start()
            x_copy(c, 3).start()

    def q_right(c, d):
        cut = part_of(c)
        src = q_hbm.at[:, :, cut] if d == 0 else qbuf.at[d, :, :, cut]
        return remote(
            src, qbuf.at[d + 1, :, :, cut], qs_sem.at[c, d], qr_sem.at[c, d + 1], right
        )

    def q_left(c, d):
        cut = part_of(c)
        src = q_hbm.at[:, :, cut] if d == 0 else qbuf.at[d, :, :, cut]
        to = (d if d else n) - 1
        return remote(
            src, qbuf.at[to, :, :, cut], qs_sem.at[c, d if d else n], qr_sem.at[c, to], left
        )

    def q_moves(d):
        if d == 0:
            return [(has_right, q_right), (has_left, q_left)]
        moves = []
        if d < n - 1:
            moves.append(((d <= me) & has_right, q_right))
        if d > 1:
            moves.append(((d > me) & has_left, q_left))
        return moves

    def send_queries(c, d):
        for flag, make in q_moves(d):
            pl.when(flag)(lambda make=make: make(c, d).start())

    def take_queries(c, d):
        cut = part_of(c)
        held = qbuf.at[d, :, :, cut]
        remote(held, held, qs_sem.at[c, d], qr_sem.at[c, d], right).wait_recv()
        send_queries(c, d)

    icopies = [None] + [
        remote(idbuf.at[0], idbuf.at[d], is_sem.at[d], ir_sem.at[d], ahead[d]) for d in range(1, n)
    ]
    for copy in icopies[1:]:
        copy.start()
    send_queries(0, 0)
    x_keys(0)
    for c in range(1, chunks):
        send_queries(c, 0)
    x_values(0)

    slots = [n - 1, 0, 1] + far_slots
    banded_width, all_width = 3 * tokens, n * tokens
    here = slice(tokens, 2 * tokens)

    def grid(width, axis):
        return lax.broadcasted_iota(jnp.int32, (frame_count, row_count, width), axis)

    def same_row(width):
        return grid(width, 1) == grid(width, 2) % row_count

    def same_frame():
        return grid(tokens, 0) == grid(tokens, 2) // row_count

    def in_band():
        keys = lax.broadcasted_iota(jnp.int32, (frame_count, banded_width), 0)
        lane = lax.broadcasted_iota(jnp.int32, (frame_count, banded_width), 1)
        block, frame = lane // tokens, lane % tokens // row_count
        return (
            ((block == 0) & (keys >= frame)) | (block == 1) | ((block == 2) & (keys <= frame))
        )

    def heads_of(c):
        return [(h, pl.ds(h * HEAD_DIM, HEAD_DIM)) for h in range(c * per_chunk, (c + 1) * per_chunk)]

    def side_by_side(rows):
        return jnp.concatenate(rows, axis=1)

    def score_block(c):
        chosen = side_by_side([idbuf[d][0:1] for d in slots])
        for h, cut in heads_of(c):
            query = jnp.concatenate(
                [qbuf[d, :, :, cut].reshape(tokens, HEAD_DIM) for d in slots], axis=0
            )
            image_keys = rbuf[0, :, :, cut].reshape(images * span, HEAD_DIM)
            both = scores_of(image_keys, query)
            score = both[0:span]
            for i in range(1, images):
                score = jnp.where(chosen == i, both[i * span : (i + 1) * span], score)
            score = score * factor
            keys = kvbuf[0, 0, :, :, cut].reshape(tokens, HEAD_DIM)
            near = scores_of(keys, query[0:banded_width]) * factor
            near = near.reshape(frame_count, row_count, banded_width)
            time = jnp.sum(jnp.where(same_row(banded_width), near, 0.0), axis=1)
            time = jnp.where(in_band(), time, NEG)
            time_top = jnp.max(time, axis=0, keepdims=True)
            time = jnp.exp(time - time_top)
            ptime[h] = time
            time_sum = jnp.sum(time, axis=0, keepdims=True)
            other_keys = kvbuf[1, 0, :, :, cut].reshape(tokens, HEAD_DIM)
            other = scores_of(other_keys, query[here]) * factor
            other = other.reshape(frame_count, row_count, tokens)
            frame = jnp.concatenate(
                [
                    jnp.sum(jnp.where(same_frame(), near[:, :, here], 0.0), axis=0),
                    jnp.sum(jnp.where(same_frame(), other, 0.0), axis=0),
                ],
                axis=0,
            )
            top = jnp.max(score, axis=0, keepdims=True)
            frame_top = jnp.max(frame, axis=0, keepdims=True)
            top = side_by_side(
                [
                    top[:, 0:tokens],
                    jnp.maximum(top[:, here], frame_top),
                    top[:, 2 * tokens :],
                ]
            )
            frame = jnp.exp(frame - top[:, here])
            pframe[h] = frame
            frame_sum = jnp.sum(frame, axis=0, keepdims=True)
            score = jnp.exp(score - top)
            pref[h] = score
            total = jnp.sum(score, axis=0, keepdims=True)
            for i, d in enumerate(slots):
                at = slice(i * tokens, (i + 1) * tokens)
                rows = [top[:, at], total[:, at] + frame_sum if d == 0 else total[:, at]]
                if d in banded:
                    rows += [time_top[:, at], time_sum[:, at]]
                else:
                    rows += [jnp.zeros((2, tokens), jnp.float32)]
                stats[0, c, d, h % per_chunk] = jnp.concatenate(rows, axis=0)

    def scale_of(c, d, h, k):
        tops, sums = [], []
        for e in range(n):
            place = (d - e) % n
            if k == 2 and place not in banded:
                continue
            block = stats[e, c, place, h % per_chunk]
            tops.append(block[k : k + 1])
            sums.append(block[k + 1 : k + 2])
        top = functools.reduce(jnp.maximum, tops)
        total = sum(s * jnp.exp(t - top) for t, s in zip(tops, sums))
        return jnp.exp(tops[0] - top) / total

    def value_block(c):
        chosen = side_by_side([idbuf[d][0:1] for d in slots])
        for h, cut in heads_of(c):
            scale = side_by_side([scale_of(c, d, h, 0) for d in slots])
            weight = pref[h] * scale
            weight = jnp.concatenate(
                [jnp.where(chosen == i, weight, 0.0).astype(jnp.bfloat16) for i in range(images)],
                axis=0,
            )
            start = images * span
            result = jnp.dot(vt[h, :, 0:start], weight, preferred_element_type=jnp.float32)
            time = ptime[h] * side_by_side([scale_of(c, d, h, 2) for d in slots[:3]])
            time = jnp.where(same_row(banded_width), time[:, None, :], 0.0)
            time = time.reshape(tokens, banded_width).astype(jnp.bfloat16)
            timed = jnp.dot(
                vt[h, :, start : start + tokens], time, preferred_element_type=jnp.float32
            )
            frame = pframe[h] * scale[:, here]
            frames = [
                jnp.where(same_frame(), frame[i * row_count : (i + 1) * row_count][None], 0.0)
                .reshape(tokens, tokens)
                .astype(jnp.bfloat16)
                for i in range(2)
            ]
            framed = jnp.dot(
                vt[h, :, start : start + 2 * tokens],
                jnp.concatenate(frames, axis=0),
                preferred_element_type=jnp.float32,
            )
            for i, d in enumerate(slots):
                at = slice(i * tokens, (i + 1) * tokens)
                piece = result[:, at]
                if d in banded:
                    piece = piece + timed[:, at]
                if d == 0:
                    piece = piece + framed
                mine[d, h] = piece

    def turn_values(c):
        for h, cut in heads_of(c):
            blocks = [
                rbuf[1, :, :, cut].reshape(images * span, HEAD_DIM),
                kvbuf[0, 1, :, :, cut].reshape(tokens, HEAD_DIM),
                kvbuf[1, 1, :, :, cut].reshape(tokens, HEAD_DIM),
            ]
            values = jnp.concatenate(blocks, axis=0).astype(jnp.float32)
            vt[h] = values.T.astype(jnp.bfloat16)

    def stats_copy(c, d):
        return remote(stats.at[0, c], stats.at[d, c], ss_sem.at[c, d], sr_sem.at[c, d], ahead[d])

    def p_left(c, d):
        held = pl.ds(c * per_chunk, per_chunk)
        return remote(
            part.at[d, held], got.at[d - 1, held], ps_sem.at[c, d], pr_sem.at[c, d - 1], left
        )

    def p_right(c, d):
        held = pl.ds(c * per_chunk, per_chunk)
        return remote(
            part.at[d, held], got.at[d + 1, held], ps_sem.at[c, d], pr_sem.at[c, d + 1], right
        )

    def p_wait(c, d):
        held = got.at[d, pl.ds(c * per_chunk, per_chunk)]
        remote(held, held, ps_sem.at[c, 0], pr_sem.at[c, d], right).wait_recv()

    def pass_on(c, d, gather):
        heads = [h for h, _ in heads_of(c)]
        if gather:
            p_wait(c, d)
        for h in heads:
            total = mine[d, h]
            if gather:
                total = total + got[d, h].astype(jnp.float32)
            part[d, h] = total.astype(jnp.bfloat16)
        pl.when(d <= me)(lambda: p_left(c, d).start())
        pl.when(d > me)(lambda: p_right(c, d).start())

    chain = far_slots + [n - 1, 1]

    def take_near(c):
        if c < chunks:
            take_queries(c, 1)
            take_queries(c, n - 1)

    def take_far(c):
        if c < chunks:
            for d in far_slots:
                take_queries(c, d)

    def scores(c):
        x_copy(c, 0).wait_recv()
        x_copy(c, 1).wait_recv()
        score_block(c)
        for d in range(1, n):
            stats_copy(c, d).start()

    def values(c):
        x_copy(c, 2).wait_recv()
        x_copy(c, 3).wait_recv()
        turn_values(c)
        for d in range(1, n):
            stats_copy(c, d).wait_recv()
        value_block(c)

        @pl.when(jnp.logical_not(middle))
        def _():
            for d in chain:
                pass_on(c, d, False)

    def combine(c):
        @pl.when(middle)
        def _():
            for d in chain:
                pass_on(c, d, True)

    def finish(c):
        pl.when(has_right)(lambda: p_wait(c, 0))
        pl.when(has_left)(lambda: p_wait(c, n))
        for h, cut in heads_of(c):
            total = mine[0, h]
            total = total + jnp.where(has_right, got[0, h].astype(jnp.float32), 0.0)
            total = total + jnp.where(has_left, got[n, h].astype(jnp.float32), 0.0)
            out_ref[:, :, cut] = total.T.reshape(frame_count, row_count, HEAD_DIM).astype(
                jnp.bfloat16
            )

    got[0] = jnp.zeros_like(got[0])
    got[n] = jnp.zeros_like(got[n])
    for copy in loads:
        copy.wait()
    for d in range(1, n):
        icopies[d].wait_recv()
    take_near(0)
    x_keys(1)
    take_far(0)
    take_near(1)
    x_values(1)
    for c in range(chunks):
        scores(c)
        take_far(c + 1)
        take_near(c + 2)
        x_keys(c + 2)
        x_values(c + 2)
        if c >= 2:
            combine(c - 2)
        if c >= 1:
            values(c - 1)
    if chunks >= 2:
        combine(chunks - 2)
    values(chunks - 1)
    combine(chunks - 1)
    for c in range(chunks):
        finish(c)

    for copy in icopies[1:]:
        copy.wait_send()
    for c in range(chunks):
        for k in range(4):
            x_copy(c, k).wait_send()
        for d in range(n):
            for flag, make in q_moves(d):
                pl.when(flag)(lambda make=make: make(c, d).wait_send())
        for d in range(1, n):
            stats_copy(c, d).wait_send()
            held = part.at[d, pl.ds(c * per_chunk, per_chunk)]
            remote(held, held, ps_sem.at[c, d], pr_sem.at[c, d], right).wait_send()


def local_kernel(tok_q, tok_kv, ref_kv, ref_ids):
    n = lax.axis_size("frames")
    frame_count, row_count, width = tok_q.shape
    heads = width // HEAD_DIM
    chunks = heads // 2
    tokens = frame_count * row_count
    images, ref_rows = ref_kv.shape[1:3]
    span = 2 * ref_rows
    dma = pltpu.SemaphoreType.DMA
    in_hbm = pl.BlockSpec(memory_space=pltpu.HBM)
    return pl.pallas_call(
        functools.partial(kernel, n, chunks),
        out_shape=jax.ShapeDtypeStruct(tok_q.shape, jnp.bfloat16),
        in_specs=[in_hbm] * 3 + [pl.BlockSpec(memory_space=pltpu.SMEM)],
        out_specs=pl.BlockSpec(memory_space=pltpu.VMEM),
        scratch_shapes=[
            pltpu.VMEM((n,) + tok_q.shape, jnp.bfloat16),
            pltpu.VMEM((2,) + tok_kv.shape, jnp.bfloat16),
            pltpu.VMEM((2, images, span, width), jnp.bfloat16),
            pltpu.VMEM((n, 8, tokens), jnp.int32),
            pltpu.VMEM((heads, span, n * tokens), jnp.float32),
            pltpu.VMEM((heads, frame_count, 3 * tokens), jnp.float32),
            pltpu.VMEM((heads, 2 * row_count, tokens), jnp.float32),
            pltpu.VMEM((n, chunks, n, heads // chunks, 4, tokens), jnp.float32),
            pltpu.VMEM((heads, HEAD_DIM, images * span + 2 * tokens), jnp.bfloat16),
            pltpu.VMEM((n, heads, HEAD_DIM, tokens), jnp.float32),
            pltpu.VMEM((n, heads, HEAD_DIM, tokens), jnp.bfloat16),
            pltpu.VMEM((n + 1, heads, HEAD_DIM, tokens), jnp.bfloat16),
            dma((4,)),
            dma((chunks, 4)),
            dma((chunks, 4)),
            dma((chunks, n + 1)),
            dma((chunks, n)),
            dma((n,)),
            dma((n,)),
            dma((chunks, n)),
            dma((chunks, n)),
            dma((chunks, n)),
            dma((chunks, n + 1)),
        ],
        compiler_params=pltpu.CompilerParams(
            collective_id=0, has_side_effects=True, vmem_limit_bytes=64 * 1024 * 1024
        ),
    )(tok_q, tok_kv, ref_kv, ref_ids)


def local(tok_q, tok_kv, ref_kv, ref_ids):
    frame_count, row_count, width = tok_q.shape
    fits = (
        3 <= lax.axis_size("frames") <= 4
        and lax.axis_size("rows") == 2
        and frame_count == BAND
        and row_count % 16 == 0
        and frame_count * row_count == 128
        and ref_kv.shape[2] % 16 == 0
        and (width // HEAD_DIM) % 2 == 0
    )
    return (local_kernel if fits else local_general)(tok_q, tok_kv, ref_kv, ref_ids)


def solution(mesh):
    placed = (
        P(("clip", "frames"), "rows", "heads"),
        P(None, ("clip", "frames"), "rows", "heads"),
        P(None, "clip", ("frames", "rows"), "heads"),
        P(("clip", "frames")),
    )
    return jax.shard_map(
        local,
        mesh=mesh,
        in_specs=placed,
        out_specs=P(("clip", "frames"), "rows", "heads"),
        check_vma=False,
    )
```

```python
import functools

import jax
import jax.numpy as jnp
from jax import lax
from jax.experimental import pallas as pl
from jax.experimental.pallas import tpu as pltpu
from jax.sharding import PartitionSpec as P

HEAD_DIM = 128
BAND = 8


def padded_2(value, sides, width):
    for axis, dim in sides:
        devices, length = (lax.axis_size(axis), value.shape[dim])
        up = [(i, (i + 1) % devices) for i in range(devices)]
        down = [(j, i) for i, j in up]
        last = lax.slice_in_dim(value, length - width, length, axis=dim)
        first = lax.slice_in_dim(value, 0, width, axis=dim)
        before = lax.ppermute(last, axis, up)
        after = lax.ppermute(first, axis, down)
        value = jnp.concatenate([before, value, after], axis=dim)
    return value


def attend_frame(query, frame_keys, frame_values, image_keys, image_values, factor):
    local_scores = (
        jnp.einsum("thd,shd->hts", query, frame_keys, preferred_element_type=jnp.float32) * factor
    )
    image_scores = (
        jnp.einsum("thd,shd->hts", query, image_keys, preferred_element_type=jnp.float32) * factor
    )
    top = jnp.maximum(jnp.max(local_scores, axis=-1), jnp.max(image_scores, axis=-1))
    local_exp = jnp.exp(local_scores - top[..., None])
    image_exp = jnp.exp(image_scores - top[..., None])
    total = jnp.sum(local_exp, axis=-1) + jnp.sum(image_exp, axis=-1)
    local_weights = (local_exp / total[..., None]).astype(jnp.bfloat16)
    image_weights = (image_exp / total[..., None]).astype(jnp.bfloat16)
    result = jnp.einsum(
        "hts,shd->thd", local_weights, frame_values, preferred_element_type=jnp.float32
    )
    result = result + jnp.einsum(
        "hts,shd->thd", image_weights, image_values, preferred_element_type=jnp.float32
    )
    return result


def local_general(tok_q, tok_kv, ref_kv, ref_ids):
    frame_count, row_count, feat_width = tok_q.shape
    head_count = feat_width // HEAD_DIM
    factor = 1.0 / HEAD_DIM**0.5
    query_heads = tok_q.reshape(frame_count, row_count, head_count, HEAD_DIM)
    padded = padded_2(tok_kv, (("frames", 1),), BAND)
    band_scores = []
    for offset in range(2 * BAND + 1):
        key_block = padded[0, offset : offset + frame_count].reshape(
            frame_count, row_count, head_count, HEAD_DIM
        )
        band_scores.append(
            jnp.einsum("frhd,frhd->frh", query_heads, key_block, preferred_element_type=jnp.float32)
            * factor
        )
    band_weights = jax.nn.softmax(jnp.stack(band_scores), axis=0).astype(jnp.bfloat16)
    temporal = jnp.zeros((frame_count, row_count, head_count, HEAD_DIM), jnp.float32)
    for offset in range(2 * BAND + 1):
        value_block = padded[1, offset : offset + frame_count].reshape(
            frame_count, row_count, head_count, HEAD_DIM
        )
        temporal = temporal + jnp.einsum(
            "frh,frhd->frhd", band_weights[offset], value_block, preferred_element_type=jnp.float32
        )
    temporal = temporal.reshape(frame_count, row_count, feat_width)
    references = lax.all_gather(ref_kv, ("frames", "rows"), axis=2, tiled=True)
    ref_length = references.shape[2]

    def spatial_frame(inputs):
        query_frame, keys_frame, values_frame, image_id = inputs
        chosen = lax.dynamic_index_in_dim(references, image_id, axis=1, keepdims=False)
        image_keys = chosen[0].reshape(ref_length, head_count, HEAD_DIM)
        image_values = chosen[1].reshape(ref_length, head_count, HEAD_DIM)
        queries = query_frame.reshape(query_frame.shape[0], head_count, HEAD_DIM)
        keys_full = keys_frame.reshape(keys_frame.shape[0], head_count, HEAD_DIM)
        values_full = values_frame.reshape(values_frame.shape[0], head_count, HEAD_DIM)
        result = attend_frame(queries, keys_full, values_full, image_keys, image_values, factor)
        return result.reshape(query_frame.shape[0], feat_width)

    query_moved, pairs_moved = (
        lax.all_to_all(tok_q[None], "rows", split_axis=1, concat_axis=2, tiled=True),
        lax.all_to_all(tok_kv, "rows", split_axis=1, concat_axis=2, tiled=True),
    )
    per_device = frame_count // lax.axis_size("rows")
    local_ids = lax.dynamic_slice_in_dim(ref_ids, lax.axis_index("rows") * per_device, per_device)
    attended = lax.map(spatial_frame, (query_moved[0], pairs_moved[0], pairs_moved[1], local_ids))
    spatial = lax.all_to_all(attended, "rows", split_axis=1, concat_axis=0, tiled=True)
    return (temporal + spatial).astype(jnp.bfloat16)


NEG = -1e30
MESH = pl.DeviceIdType.MESH


def scores_of(keys, queries):
    return lax.dot_general(
        keys, queries, (((1,), (1,)), ((), ())), preferred_element_type=jnp.float32
    )


def kernel(
    n,
    chunks,
    q_hbm,
    kv_hbm,
    ref_hbm,
    ids_ref,
    out_ref,
    qbuf,
    kvbuf,
    rbuf,
    idbuf,
    pref,
    ptime,
    pframe,
    stats,
    vt,
    mine,
    part,
    got,
    local_sem,
    xs_sem,
    xr_sem,
    qs_sem,
    qr_sem,
    is_sem,
    ir_sem,
    ss_sem,
    sr_sem,
    ps_sem,
    pr_sem,
):
    frame_count, row_count, width = q_hbm.shape
    head_count = width // HEAD_DIM
    per_chunk = head_count // chunks
    chunk_width = per_chunk * HEAD_DIM
    tokens = frame_count * row_count
    images, ref_rows = ref_hbm.shape[1], ref_hbm.shape[2]
    span = 2 * ref_rows
    factor = 1.0 / HEAD_DIM**0.5
    me = lax.axis_index("frames")
    has_left, has_right = me >= 1, me <= n - 2
    middle = has_left & has_right
    across = {"rows": 1 - lax.axis_index("rows")}
    ahead = [{"frames": lax.rem(me + d, n)} for d in range(n)]
    right, left = ahead[1], ahead[n - 1]
    banded = (0, 1, n - 1)
    far_slots = list(range(2, n - 1))
    own_rows, far_rows = pl.ds(0, ref_rows), pl.ds(ref_rows, ref_rows)

    loads = [
        pltpu.make_async_copy(q_hbm, qbuf.at[0], local_sem.at[0]),
        pltpu.make_async_copy(ref_hbm.at[0], rbuf.at[0, :, own_rows], local_sem.at[1]),
        pltpu.make_async_copy(kv_hbm, kvbuf.at[0], local_sem.at[2]),
        pltpu.make_async_copy(ref_hbm.at[1], rbuf.at[1, :, own_rows], local_sem.at[3]),
    ]
    for copy in loads:
        copy.start()

    barrier = pltpu.get_barrier_semaphore()
    for d in range(1, n):
        pl.semaphore_signal(barrier, inc=1, device_id=ahead[d], device_id_type=MESH)
    pl.semaphore_signal(barrier, inc=1, device_id=across, device_id_type=MESH)

    lane_frame = lax.broadcasted_iota(jnp.int32, (8, tokens), 1) // row_count
    which = jnp.zeros((8, tokens), jnp.int32)
    for f in range(frame_count):
        which = jnp.where(lane_frame == f, ids_ref[f], which)
    idbuf[0] = which

    pl.semaphore_wait(barrier, n)

    def remote(src, dst, send, recv, where):
        return pltpu.make_async_remote_copy(
            src_ref=src, dst_ref=dst, send_sem=send, recv_sem=recv,
            device_id=where, device_id_type=MESH,
        )

    def part_of(c):
        return pl.ds(c * chunk_width, chunk_width)

    def x_copy(c, k):
        cut = part_of(c)
        if k % 2 == 0:
            src, dst = ref_hbm.at[k // 2, :, :, cut], rbuf.at[k // 2, :, far_rows, cut]
        else:
            src, dst = kv_hbm.at[k // 2, :, :, cut], kvbuf.at[1, k // 2, :, :, cut]
        return remote(src, dst, xs_sem.at[c, k], xr_sem.at[c, k], across)

    def q_right(c, d):
        cut = part_of(c)
        src = q_hbm.at[:, :, cut] if d == 0 else qbuf.at[d, :, :, cut]
        return remote(
            src, qbuf.at[d + 1, :, :, cut], qs_sem.at[c, d], qr_sem.at[c, d + 1], right
        )

    def q_left(c, d):
        cut = part_of(c)
        src = q_hbm.at[:, :, cut] if d == 0 else qbuf.at[d, :, :, cut]
        to = (d if d else n) - 1
        return remote(
            src, qbuf.at[to, :, :, cut], qs_sem.at[c, d if d else n], qr_sem.at[c, to], left
        )

    def q_moves(d):
        if d == 0:
            return [(has_right, q_right), (has_left, q_left)]
        moves = []
        if d < n - 1:
            moves.append(((d <= me) & has_right, q_right))
        if d > 1:
            moves.append(((d > me) & has_left, q_left))
        return moves

    def send_queries(c, d):
        for flag, make in q_moves(d):
            pl.when(flag)(lambda make=make: make(c, d).start())

    def take_queries(c, d):
        cut = part_of(c)
        held = qbuf.at[d, :, :, cut]
        remote(held, held, qs_sem.at[c, d], qr_sem.at[c, d], right).wait_recv()
        send_queries(c, d)

    icopies = [None] + [
        remote(idbuf.at[0], idbuf.at[d], is_sem.at[d], ir_sem.at[d], ahead[d]) for d in range(1, n)
    ]
    for copy in icopies[1:]:
        copy.start()
    for c in range(chunks):
        send_queries(c, 0)
        for k in range(4):
            x_copy(c, k).start()

    slots = [n - 1, 0, 1] + far_slots
    banded_width, all_width = 3 * tokens, n * tokens
    here = slice(tokens, 2 * tokens)

    def grid(width, axis):
        return lax.broadcasted_iota(jnp.int32, (frame_count, row_count, width), axis)

    lane = lax.broadcasted_iota(jnp.int32, (1, banded_width), 1)
    lane_row, lane_block = lax.rem(lane, row_count), lax.div(lane, tokens)
    band_frame = lax.div(lax.rem(lane, tokens), row_count)
    lane_low = jnp.where(lane_block == 0, band_frame, 0)
    lane_high = jnp.where(lane_block == 2, band_frame, frame_count)

    def same_row(width):
        return grid(width, 1) == lane_row[None]

    def same_frame():
        return grid(tokens, 0) == band_frame[None, :, here]

    def in_band():
        keys = lax.broadcasted_iota(jnp.int32, (frame_count, banded_width), 0)
        return (keys >= lane_low) & (keys <= lane_high)

    def heads_of(c):
        return [(h, pl.ds(h * HEAD_DIM, HEAD_DIM)) for h in range(c * per_chunk, (c + 1) * per_chunk)]

    def side_by_side(rows):
        return jnp.concatenate(rows, axis=1)

    def score_block(c):
        chosen = side_by_side([idbuf[d][0:1] for d in slots])
        for h, cut in heads_of(c):
            query = jnp.concatenate(
                [qbuf[d, :, :, cut].reshape(tokens, HEAD_DIM) for d in slots], axis=0
            )
            image_keys = rbuf[0, :, :, cut].reshape(images * span, HEAD_DIM)
            both = scores_of(image_keys, query)
            score = both[0:span]
            for i in range(1, images):
                score = jnp.where(chosen == i, both[i * span : (i + 1) * span], score)
            score = score * factor
            keys = kvbuf[0, 0, :, :, cut].reshape(tokens, HEAD_DIM)
            near = scores_of(keys, query[0:banded_width]) * factor
            near = near.reshape(frame_count, row_count, banded_width)
            time = jnp.sum(jnp.where(same_row(banded_width), near, 0.0), axis=1)
            time = jnp.where(in_band(), time, NEG)
            time_top = jnp.max(time, axis=0, keepdims=True)
            time = jnp.exp(time - time_top)
            ptime[h] = time
            time_sum = jnp.sum(time, axis=0, keepdims=True)
            other_keys = kvbuf[1, 0, :, :, cut].reshape(tokens, HEAD_DIM)
            other = scores_of(other_keys, query[here]) * factor
            other = other.reshape(frame_count, row_count, tokens)
            frame = jnp.concatenate(
                [
                    jnp.sum(jnp.where(same_frame(), near[:, :, here], 0.0), axis=0),
                    jnp.sum(jnp.where(same_frame(), other, 0.0), axis=0),
                ],
                axis=0,
            )
            top = jnp.max(score, axis=0, keepdims=True)
            frame_top = jnp.max(frame, axis=0, keepdims=True)
            top = side_by_side(
                [
                    top[:, 0:tokens],
                    jnp.maximum(top[:, here], frame_top),
                    top[:, 2 * tokens :],
                ]
            )
            frame = jnp.exp(frame - top[:, here])
            pframe[h] = frame
            frame_sum = jnp.sum(frame, axis=0, keepdims=True)
            score = jnp.exp(score - top)
            pref[h] = score
            total = jnp.sum(score, axis=0, keepdims=True)
            for i, d in enumerate(slots):
                at = slice(i * tokens, (i + 1) * tokens)
                rows = [top[:, at], total[:, at] + frame_sum if d == 0 else total[:, at]]
                if d in banded:
                    rows += [time_top[:, at], time_sum[:, at]]
                else:
                    rows += [jnp.zeros((2, tokens), jnp.float32)]
                stats[0, c, d, h % per_chunk] = jnp.concatenate(rows, axis=0)

    def scale_of(c, d, h, k):
        tops, sums = [], []
        for e in range(n):
            place = (d - e) % n
            if k == 2 and place not in banded:
                continue
            block = stats[e, c, place, h % per_chunk]
            tops.append(block[k : k + 1])
            sums.append(block[k + 1 : k + 2])
        top = functools.reduce(jnp.maximum, tops)
        total = sum(s * jnp.exp(t - top) for t, s in zip(tops, sums))
        return jnp.exp(tops[0] - top) / total

    def value_block(c):
        chosen = side_by_side([idbuf[d][0:1] for d in slots])
        for h, cut in heads_of(c):
            scale = side_by_side([scale_of(c, d, h, 0) for d in slots])
            weight = pref[h] * scale
            weight = jnp.concatenate(
                [jnp.where(chosen == i, weight, 0.0).astype(jnp.bfloat16) for i in range(images)],
                axis=0,
            )
            start = images * span
            result = jnp.dot(vt[h, :, 0:start], weight, preferred_element_type=jnp.float32)
            time = ptime[h] * side_by_side([scale_of(c, d, h, 2) for d in slots[:3]])
            time = jnp.where(same_row(banded_width), time[:, None, :], 0.0)
            time = time.reshape(tokens, banded_width).astype(jnp.bfloat16)
            timed = jnp.dot(
                vt[h, :, start : start + tokens], time, preferred_element_type=jnp.float32
            )
            frame = pframe[h] * scale[:, here]
            frames = [
                jnp.where(same_frame(), frame[i * row_count : (i + 1) * row_count][None], 0.0)
                .reshape(tokens, tokens)
                .astype(jnp.bfloat16)
                for i in range(2)
            ]
            framed = jnp.dot(
                vt[h, :, start : start + 2 * tokens],
                jnp.concatenate(frames, axis=0),
                preferred_element_type=jnp.float32,
            )
            for i, d in enumerate(slots):
                at = slice(i * tokens, (i + 1) * tokens)
                piece = result[:, at]
                if d in banded:
                    piece = piece + timed[:, at]
                if d == 0:
                    piece = piece + framed
                mine[d, h] = piece

    def turn_values(c):
        for h, cut in heads_of(c):
            blocks = [
                rbuf[1, :, :, cut].reshape(images * span, HEAD_DIM),
                kvbuf[0, 1, :, :, cut].reshape(tokens, HEAD_DIM),
                kvbuf[1, 1, :, :, cut].reshape(tokens, HEAD_DIM),
            ]
            values = jnp.concatenate(blocks, axis=0).astype(jnp.float32)
            vt[h] = values.T.astype(jnp.bfloat16)

    def stats_copy(c, d):
        return remote(stats.at[0, c], stats.at[d, c], ss_sem.at[c, d], sr_sem.at[c, d], ahead[d])

    def p_left(c, d):
        held = pl.ds(c * per_chunk, per_chunk)
        return remote(
            part.at[d, held], got.at[d - 1, held], ps_sem.at[c, d], pr_sem.at[c, d - 1], left
        )

    def p_right(c, d):
        held = pl.ds(c * per_chunk, per_chunk)
        return remote(
            part.at[d, held], got.at[d + 1, held], ps_sem.at[c, d], pr_sem.at[c, d + 1], right
        )

    def p_wait(c, d):
        held = got.at[d, pl.ds(c * per_chunk, per_chunk)]
        remote(held, held, ps_sem.at[c, 0], pr_sem.at[c, d], right).wait_recv()

    def pass_on(c, d, gather):
        heads = [h for h, _ in heads_of(c)]
        if gather:
            p_wait(c, d)
        for h in heads:
            total = mine[d, h]
            if gather:
                total = total + got[d, h].astype(jnp.float32)
            part[d, h] = total.astype(jnp.bfloat16)
        pl.when(d <= me)(lambda: p_left(c, d).start())
        pl.when(d > me)(lambda: p_right(c, d).start())

    chain = far_slots + [n - 1, 1]

    def scores(c):
        for d in [1, n - 1] + far_slots:
            take_queries(c, d)
        x_copy(c, 0).wait_recv()
        x_copy(c, 1).wait_recv()
        score_block(c)
        for d in range(1, n):
            stats_copy(c, d).start()

    def values(c):
        x_copy(c, 2).wait_recv()
        x_copy(c, 3).wait_recv()
        turn_values(c)
        for d in range(1, n):
            stats_copy(c, d).wait_recv()
        value_block(c)

        @pl.when(jnp.logical_not(middle))
        def _():
            for d in chain:
                pass_on(c, d, False)

    def combine(c):
        @pl.when(middle)
        def _():
            for d in chain:
                pass_on(c, d, True)

    def finish(c):
        pl.when(has_right)(lambda: p_wait(c, 0))
        pl.when(has_left)(lambda: p_wait(c, n))
        for h, cut in heads_of(c):
            total = mine[0, h]
            total = total + jnp.where(has_right, got[0, h].astype(jnp.float32), 0.0)
            total = total + jnp.where(has_left, got[n, h].astype(jnp.float32), 0.0)
            out_ref[:, :, cut] = total.T.reshape(frame_count, row_count, HEAD_DIM).astype(
                jnp.bfloat16
            )

    got[0] = jnp.zeros_like(got[0])
    got[n] = jnp.zeros_like(got[n])
    for copy in loads:
        copy.wait()
    for d in range(1, n):
        icopies[d].wait_recv()
    scores(0)
    for c in range(chunks):
        if c + 1 < chunks:
            scores(c + 1)
        if c >= 1:
            combine(c - 1)
        values(c)
    combine(chunks - 1)
    for c in range(chunks):
        finish(c)

    for copy in icopies[1:]:
        copy.wait_send()
    for c in range(chunks):
        for k in range(4):
            x_copy(c, k).wait_send()
        for d in range(n):
            for flag, make in q_moves(d):
                pl.when(flag)(lambda make=make: make(c, d).wait_send())
        for d in range(1, n):
            stats_copy(c, d).wait_send()
            held = part.at[d, pl.ds(c * per_chunk, per_chunk)]
            remote(held, held, ps_sem.at[c, d], pr_sem.at[c, d], right).wait_send()


def local_kernel(tok_q, tok_kv, ref_kv, ref_ids):
    n = lax.axis_size("frames")
    frame_count, row_count, width = tok_q.shape
    heads = width // HEAD_DIM
    chunks = heads // 2
    tokens = frame_count * row_count
    images, ref_rows = ref_kv.shape[1:3]
    span = 2 * ref_rows
    dma = pltpu.SemaphoreType.DMA
    in_hbm = pl.BlockSpec(memory_space=pltpu.HBM)
    return pl.pallas_call(
        functools.partial(kernel, n, chunks),
        out_shape=jax.ShapeDtypeStruct(tok_q.shape, jnp.bfloat16),
        in_specs=[in_hbm] * 3 + [pl.BlockSpec(memory_space=pltpu.SMEM)],
        out_specs=pl.BlockSpec(memory_space=pltpu.VMEM),
        scratch_shapes=[
            pltpu.VMEM((n,) + tok_q.shape, jnp.bfloat16),
            pltpu.VMEM((2,) + tok_kv.shape, jnp.bfloat16),
            pltpu.VMEM((2, images, span, width), jnp.bfloat16),
            pltpu.VMEM((n, 8, tokens), jnp.int32),
            pltpu.VMEM((heads, span, n * tokens), jnp.float32),
            pltpu.VMEM((heads, frame_count, 3 * tokens), jnp.float32),
            pltpu.VMEM((heads, 2 * row_count, tokens), jnp.float32),
            pltpu.VMEM((n, chunks, n, heads // chunks, 4, tokens), jnp.float32),
            pltpu.VMEM((heads, HEAD_DIM, images * span + 2 * tokens), jnp.bfloat16),
            pltpu.VMEM((n, heads, HEAD_DIM, tokens), jnp.float32),
            pltpu.VMEM((n, heads, HEAD_DIM, tokens), jnp.bfloat16),
            pltpu.VMEM((n + 1, heads, HEAD_DIM, tokens), jnp.bfloat16),
            dma((4,)),
            dma((chunks, 4)),
            dma((chunks, 4)),
            dma((chunks, n + 1)),
            dma((chunks, n)),
            dma((n,)),
            dma((n,)),
            dma((chunks, n)),
            dma((chunks, n)),
            dma((chunks, n)),
            dma((chunks, n + 1)),
        ],
        compiler_params=pltpu.CompilerParams(
            collective_id=0, has_side_effects=True, vmem_limit_bytes=64 * 1024 * 1024
        ),
    )(tok_q, tok_kv, ref_kv, ref_ids)


def local(tok_q, tok_kv, ref_kv, ref_ids):
    frame_count, row_count, width = tok_q.shape
    fits = (
        3 <= lax.axis_size("frames") <= 4
        and lax.axis_size("rows") == 2
        and frame_count == BAND
        and row_count % 16 == 0
        and frame_count * row_count == 128
        and ref_kv.shape[2] % 16 == 0
        and (width // HEAD_DIM) % 2 == 0
    )
    return (local_kernel if fits else local_general)(tok_q, tok_kv, ref_kv, ref_ids)


def solution(mesh):
    placed = (
        P(("clip", "frames"), "rows", "heads"),
        P(None, ("clip", "frames"), "rows", "heads"),
        P(None, "clip", ("frames", "rows"), "heads"),
        P(("clip", "frames")),
    )
    return jax.shard_map(
        local,
        mesh=mesh,
        in_specs=placed,
        out_specs=P(("clip", "frames"), "rows", "heads"),
        check_vma=False,
    )
```

```python
import functools

import jax
import jax.numpy as jnp
from jax import lax
from jax.experimental import pallas as pl
from jax.experimental.pallas import tpu as pltpu
from jax.sharding import PartitionSpec as P

HEAD_DIM = 128
BAND = 8


def padded_2(value, sides, width):
    for axis, dim in sides:
        devices, length = (lax.axis_size(axis), value.shape[dim])
        up = [(i, (i + 1) % devices) for i in range(devices)]
        down = [(j, i) for i, j in up]
        last = lax.slice_in_dim(value, length - width, length, axis=dim)
        first = lax.slice_in_dim(value, 0, width, axis=dim)
        before = lax.ppermute(last, axis, up)
        after = lax.ppermute(first, axis, down)
        value = jnp.concatenate([before, value, after], axis=dim)
    return value


def attend_frame(query, frame_keys, frame_values, image_keys, image_values, factor):
    local_scores = (
        jnp.einsum("thd,shd->hts", query, frame_keys, preferred_element_type=jnp.float32) * factor
    )
    image_scores = (
        jnp.einsum("thd,shd->hts", query, image_keys, preferred_element_type=jnp.float32) * factor
    )
    top = jnp.maximum(jnp.max(local_scores, axis=-1), jnp.max(image_scores, axis=-1))
    local_exp = jnp.exp(local_scores - top[..., None])
    image_exp = jnp.exp(image_scores - top[..., None])
    total = jnp.sum(local_exp, axis=-1) + jnp.sum(image_exp, axis=-1)
    local_weights = (local_exp / total[..., None]).astype(jnp.bfloat16)
    image_weights = (image_exp / total[..., None]).astype(jnp.bfloat16)
    result = jnp.einsum(
        "hts,shd->thd", local_weights, frame_values, preferred_element_type=jnp.float32
    )
    result = result + jnp.einsum(
        "hts,shd->thd", image_weights, image_values, preferred_element_type=jnp.float32
    )
    return result


def local_general(tok_q, tok_kv, ref_kv, ref_ids):
    frame_count, row_count, feat_width = tok_q.shape
    head_count = feat_width // HEAD_DIM
    factor = 1.0 / HEAD_DIM**0.5
    query_heads = tok_q.reshape(frame_count, row_count, head_count, HEAD_DIM)
    padded = padded_2(tok_kv, (("frames", 1),), BAND)
    band_scores = []
    for offset in range(2 * BAND + 1):
        key_block = padded[0, offset : offset + frame_count].reshape(
            frame_count, row_count, head_count, HEAD_DIM
        )
        band_scores.append(
            jnp.einsum("frhd,frhd->frh", query_heads, key_block, preferred_element_type=jnp.float32)
            * factor
        )
    band_weights = jax.nn.softmax(jnp.stack(band_scores), axis=0).astype(jnp.bfloat16)
    temporal = jnp.zeros((frame_count, row_count, head_count, HEAD_DIM), jnp.float32)
    for offset in range(2 * BAND + 1):
        value_block = padded[1, offset : offset + frame_count].reshape(
            frame_count, row_count, head_count, HEAD_DIM
        )
        temporal = temporal + jnp.einsum(
            "frh,frhd->frhd", band_weights[offset], value_block, preferred_element_type=jnp.float32
        )
    temporal = temporal.reshape(frame_count, row_count, feat_width)
    references = lax.all_gather(ref_kv, ("frames", "rows"), axis=2, tiled=True)
    ref_length = references.shape[2]

    def spatial_frame(inputs):
        query_frame, keys_frame, values_frame, image_id = inputs
        chosen = lax.dynamic_index_in_dim(references, image_id, axis=1, keepdims=False)
        image_keys = chosen[0].reshape(ref_length, head_count, HEAD_DIM)
        image_values = chosen[1].reshape(ref_length, head_count, HEAD_DIM)
        queries = query_frame.reshape(query_frame.shape[0], head_count, HEAD_DIM)
        keys_full = keys_frame.reshape(keys_frame.shape[0], head_count, HEAD_DIM)
        values_full = values_frame.reshape(values_frame.shape[0], head_count, HEAD_DIM)
        result = attend_frame(queries, keys_full, values_full, image_keys, image_values, factor)
        return result.reshape(query_frame.shape[0], feat_width)

    query_moved, pairs_moved = (
        lax.all_to_all(tok_q[None], "rows", split_axis=1, concat_axis=2, tiled=True),
        lax.all_to_all(tok_kv, "rows", split_axis=1, concat_axis=2, tiled=True),
    )
    per_device = frame_count // lax.axis_size("rows")
    local_ids = lax.dynamic_slice_in_dim(ref_ids, lax.axis_index("rows") * per_device, per_device)
    attended = lax.map(spatial_frame, (query_moved[0], pairs_moved[0], pairs_moved[1], local_ids))
    spatial = lax.all_to_all(attended, "rows", split_axis=1, concat_axis=0, tiled=True)
    return (temporal + spatial).astype(jnp.bfloat16)


NEG = -1e30
MESH = pl.DeviceIdType.MESH


def scores_of(keys, queries):
    return lax.dot_general(
        keys, queries, (((1,), (1,)), ((), ())), preferred_element_type=jnp.float32
    )


def kernel(
    n,
    chunks,
    pieces,
    q_hbm,
    kv_hbm,
    ref_hbm,
    ids_ref,
    out_ref,
    qbuf,
    kvbuf,
    rbuf,
    idbuf,
    pref,
    ptime,
    pframe,
    stats,
    vt,
    mine,
    part,
    got,
    local_sem,
    xs_sem,
    xr_sem,
    qs_sem,
    qr_sem,
    is_sem,
    ir_sem,
    ss_sem,
    sr_sem,
    ps_sem,
    pr_sem,
):
    frame_count, row_count, width = q_hbm.shape
    head_count = width // HEAD_DIM
    per_chunk = head_count // chunks
    tokens = frame_count * row_count
    images, ref_rows = ref_hbm.shape[1], ref_hbm.shape[2]
    span = 2 * ref_rows
    factor = 1.0 / HEAD_DIM**0.5
    me = lax.axis_index("frames")
    has_left, has_right = me >= 1, me <= n - 2
    middle = has_left & has_right
    across = {"rows": 1 - lax.axis_index("rows")}
    ahead = [{"frames": lax.rem(me + d, n)} for d in range(n)]
    right, left = ahead[1], ahead[n - 1]
    banded = (0, 1, n - 1)
    far_slots = list(range(2, n - 1))
    own_rows, far_rows = pl.ds(0, ref_rows), pl.ds(ref_rows, ref_rows)

    loads = [
        pltpu.make_async_copy(q_hbm, qbuf.at[0], local_sem.at[0]),
        pltpu.make_async_copy(ref_hbm.at[0], rbuf.at[0, :, own_rows], local_sem.at[1]),
        pltpu.make_async_copy(kv_hbm, kvbuf.at[0], local_sem.at[2]),
        pltpu.make_async_copy(ref_hbm.at[1], rbuf.at[1, :, own_rows], local_sem.at[3]),
    ]
    for copy in loads:
        copy.start()

    barrier = pltpu.get_barrier_semaphore()
    for d in range(1, n):
        pl.semaphore_signal(barrier, inc=1, device_id=ahead[d], device_id_type=MESH)
    pl.semaphore_signal(barrier, inc=1, device_id=across, device_id_type=MESH)

    lane_frame = lax.broadcasted_iota(jnp.int32, (8, tokens), 1) // row_count
    which = jnp.zeros((8, tokens), jnp.int32)
    for f in range(frame_count):
        which = jnp.where(lane_frame == f, ids_ref[f], which)
    idbuf[0] = which

    pl.semaphore_wait(barrier, n)

    def remote(src, dst, send, recv, where):
        return pltpu.make_async_remote_copy(
            src_ref=src, dst_ref=dst, send_sem=send, recv_sem=recv,
            device_id=where, device_id_type=MESH,
        )

    def x_copy(k):
        if k % 2 == 0:
            src, dst = ref_hbm.at[k // 2], rbuf.at[k // 2, :, far_rows]
        else:
            src, dst = kv_hbm.at[k // 2], kvbuf.at[1, k // 2]
        return remote(src, dst, xs_sem.at[k], xr_sem.at[k], across)

    def piece(p):
        count = frame_count // pieces
        return pl.ds(p * count, count)

    def q_right(p, d):
        cut = piece(p)
        src = q_hbm.at[cut] if d == 0 else qbuf.at[d, cut]
        return remote(src, qbuf.at[d + 1, cut], qs_sem.at[p, d], qr_sem.at[p, d + 1], right)

    def q_left(p, d):
        cut = piece(p)
        src = q_hbm.at[cut] if d == 0 else qbuf.at[d, cut]
        to = (d if d else n) - 1
        return remote(
            src, qbuf.at[to, cut], qs_sem.at[p, d if d else n], qr_sem.at[p, to], left
        )

    def q_moves(d):
        if d == 0:
            return [(has_right, q_right), (has_left, q_left)]
        moves = []
        if d < n - 1:
            moves.append(((d <= me) & has_right, q_right))
        if d > 1:
            moves.append(((d > me) & has_left, q_left))
        return moves

    def send_queries(p, d):
        for flag, make in q_moves(d):
            pl.when(flag)(lambda make=make: make(p, d).start())

    def take_queries(p, d):
        held = qbuf.at[d, piece(p)]
        remote(held, held, qs_sem.at[p, d], qr_sem.at[p, d], right).wait_recv()
        send_queries(p, d)

    icopies = [None] + [
        remote(idbuf.at[0], idbuf.at[d], is_sem.at[d], ir_sem.at[d], ahead[d]) for d in range(1, n)
    ]
    for copy in icopies[1:]:
        copy.start()
    x_copy(0).start()
    for p in range(pieces):
        send_queries(p, 0)
    for k in range(1, 4):
        x_copy(k).start()

    slots = [n - 1, 0, 1] + far_slots
    banded_width, all_width = 3 * tokens, n * tokens
    here = slice(tokens, 2 * tokens)

    def grid(width, axis):
        return lax.broadcasted_iota(jnp.int32, (frame_count, row_count, width), axis)

    lane = lax.broadcasted_iota(jnp.int32, (1, banded_width), 1)
    lane_row, lane_block = lax.rem(lane, row_count), lax.div(lane, tokens)
    band_frame = lax.div(lax.rem(lane, tokens), row_count)
    lane_low = jnp.where(lane_block == 0, band_frame, 0)
    lane_high = jnp.where(lane_block == 2, band_frame, frame_count)

    def same_row(width):
        return grid(width, 1) == lane_row[None]

    def same_frame():
        return grid(tokens, 0) == band_frame[None, :, here]

    def in_band():
        keys = lax.broadcasted_iota(jnp.int32, (frame_count, banded_width), 0)
        return (keys >= lane_low) & (keys <= lane_high)

    def heads_of(c):
        return [(h, pl.ds(h * HEAD_DIM, HEAD_DIM)) for h in range(c * per_chunk, (c + 1) * per_chunk)]

    def side_by_side(rows):
        return jnp.concatenate(rows, axis=1)

    def score_block(c):
        chosen = side_by_side([idbuf[d][0:1] for d in slots])
        for h, cut in heads_of(c):
            query = jnp.concatenate(
                [qbuf[d, :, :, cut].reshape(tokens, HEAD_DIM) for d in slots], axis=0
            )
            image_keys = rbuf[0, :, :, cut].reshape(images * span, HEAD_DIM)
            both = scores_of(image_keys, query)
            score = both[0:span]
            for i in range(1, images):
                score = jnp.where(chosen == i, both[i * span : (i + 1) * span], score)
            score = score * factor
            keys = kvbuf[0, 0, :, :, cut].reshape(tokens, HEAD_DIM)
            near = scores_of(keys, query[0:banded_width]) * factor
            near = near.reshape(frame_count, row_count, banded_width)
            time = jnp.sum(jnp.where(same_row(banded_width), near, 0.0), axis=1)
            time = jnp.where(in_band(), time, NEG)
            time_top = jnp.max(time, axis=0, keepdims=True)
            time = jnp.exp(time - time_top)
            ptime[h] = time
            time_sum = jnp.sum(time, axis=0, keepdims=True)
            other_keys = kvbuf[1, 0, :, :, cut].reshape(tokens, HEAD_DIM)
            other = scores_of(other_keys, query[here]) * factor
            other = other.reshape(frame_count, row_count, tokens)
            frame = jnp.concatenate(
                [
                    jnp.sum(jnp.where(same_frame(), near[:, :, here], 0.0), axis=0),
                    jnp.sum(jnp.where(same_frame(), other, 0.0), axis=0),
                ],
                axis=0,
            )
            top = jnp.max(score, axis=0, keepdims=True)
            frame_top = jnp.max(frame, axis=0, keepdims=True)
            top = side_by_side(
                [
                    top[:, 0:tokens],
                    jnp.maximum(top[:, here], frame_top),
                    top[:, 2 * tokens :],
                ]
            )
            frame = jnp.exp(frame - top[:, here])
            pframe[h] = frame
            frame_sum = jnp.sum(frame, axis=0, keepdims=True)
            score = jnp.exp(score - top)
            pref[h] = score
            total = jnp.sum(score, axis=0, keepdims=True)
            for i, d in enumerate(slots):
                at = slice(i * tokens, (i + 1) * tokens)
                rows = [top[:, at], total[:, at] + frame_sum if d == 0 else total[:, at]]
                if d in banded:
                    rows += [time_top[:, at], time_sum[:, at]]
                else:
                    rows += [jnp.zeros((2, tokens), jnp.float32)]
                stats[0, c, d, h % per_chunk] = jnp.concatenate(rows, axis=0)

    def scale_of(c, d, h, k):
        tops, sums = [], []
        for e in range(n):
            place = (d - e) % n
            if k == 2 and place not in banded:
                continue
            block = stats[e, c, place, h % per_chunk]
            tops.append(block[k : k + 1])
            sums.append(block[k + 1 : k + 2])
        top = functools.reduce(jnp.maximum, tops)
        total = sum(s * jnp.exp(t - top) for t, s in zip(tops, sums))
        return jnp.exp(tops[0] - top) / total

    def value_block(c):
        chosen = side_by_side([idbuf[d][0:1] for d in slots])
        for h, cut in heads_of(c):
            scale = side_by_side([scale_of(c, d, h, 0) for d in slots])
            weight = pref[h] * scale
            weight = jnp.concatenate(
                [jnp.where(chosen == i, weight, 0.0).astype(jnp.bfloat16) for i in range(images)],
                axis=0,
            )
            start = images * span
            result = jnp.dot(vt[h, :, 0:start], weight, preferred_element_type=jnp.float32)
            time = ptime[h] * side_by_side([scale_of(c, d, h, 2) for d in slots[:3]])
            time = jnp.where(same_row(banded_width), time[:, None, :], 0.0)
            time = time.reshape(tokens, banded_width).astype(jnp.bfloat16)
            timed = jnp.dot(
                vt[h, :, start : start + tokens], time, preferred_element_type=jnp.float32
            )
            frame = pframe[h] * scale[:, here]
            frames = [
                jnp.where(same_frame(), frame[i * row_count : (i + 1) * row_count][None], 0.0)
                .reshape(tokens, tokens)
                .astype(jnp.bfloat16)
                for i in range(2)
            ]
            framed = jnp.dot(
                vt[h, :, start : start + 2 * tokens],
                jnp.concatenate(frames, axis=0),
                preferred_element_type=jnp.float32,
            )
            for i, d in enumerate(slots):
                at = slice(i * tokens, (i + 1) * tokens)
                piece = result[:, at]
                if d in banded:
                    piece = piece + timed[:, at]
                if d == 0:
                    piece = piece + framed
                mine[d, h] = piece

    def turn_values(c):
        for h, cut in heads_of(c):
            blocks = [
                rbuf[1, :, :, cut].reshape(images * span, HEAD_DIM),
                kvbuf[0, 1, :, :, cut].reshape(tokens, HEAD_DIM),
                kvbuf[1, 1, :, :, cut].reshape(tokens, HEAD_DIM),
            ]
            values = jnp.concatenate(blocks, axis=0).astype(jnp.float32)
            vt[h] = values.T.astype(jnp.bfloat16)

    def stats_copy(c, d):
        return remote(stats.at[0, c], stats.at[d, c], ss_sem.at[c, d], sr_sem.at[c, d], ahead[d])

    def p_left(c, d):
        held = pl.ds(c * per_chunk, per_chunk)
        return remote(
            part.at[d, held], got.at[d - 1, held], ps_sem.at[c, d], pr_sem.at[c, d - 1], left
        )

    def p_right(c, d):
        held = pl.ds(c * per_chunk, per_chunk)
        return remote(
            part.at[d, held], got.at[d + 1, held], ps_sem.at[c, d], pr_sem.at[c, d + 1], right
        )

    def p_wait(c, d):
        held = got.at[d, pl.ds(c * per_chunk, per_chunk)]
        remote(held, held, ps_sem.at[c, 0], pr_sem.at[c, d], right).wait_recv()

    def pass_on(c, d, gather):
        heads = [h for h, _ in heads_of(c)]
        if gather:
            p_wait(c, d)
        for h in heads:
            total = mine[d, h]
            if gather:
                total = total + got[d, h].astype(jnp.float32)
            part[d, h] = total.astype(jnp.bfloat16)
        pl.when(d <= me)(lambda: p_left(c, d).start())
        pl.when(d > me)(lambda: p_right(c, d).start())

    chain = far_slots + [n - 1, 1]

    def scores(c):
        score_block(c)
        for d in range(1, n):
            stats_copy(c, d).start()

    def values(c):
        turn_values(c)
        for d in range(1, n):
            stats_copy(c, d).wait_recv()
        value_block(c)

        @pl.when(jnp.logical_not(middle))
        def _():
            for d in chain:
                pass_on(c, d, False)

    def combine(c):
        @pl.when(middle)
        def _():
            for d in chain:
                pass_on(c, d, True)

    def finish(c):
        pl.when(has_right)(lambda: p_wait(c, 0))
        pl.when(has_left)(lambda: p_wait(c, n))
        for h, cut in heads_of(c):
            total = mine[0, h]
            total = total + jnp.where(has_right, got[0, h].astype(jnp.float32), 0.0)
            total = total + jnp.where(has_left, got[n, h].astype(jnp.float32), 0.0)
            out_ref[:, :, cut] = total.T.reshape(frame_count, row_count, HEAD_DIM).astype(
                jnp.bfloat16
            )

    got[0] = jnp.zeros_like(got[0])
    got[n] = jnp.zeros_like(got[n])
    for copy in loads:
        copy.wait()
    for d in range(1, n):
        icopies[d].wait_recv()
    for group in ([1, n - 1], far_slots):
        for p in range(pieces):
            for d in group:
                take_queries(p, d)
    x_copy(0).wait_recv()
    x_copy(1).wait_recv()
    for c in range(chunks):
        scores(c)
    x_copy(2).wait_recv()
    x_copy(3).wait_recv()
    for c in range(chunks):
        values(c)
        if c >= 1:
            combine(c - 1)
    combine(chunks - 1)
    for c in range(chunks):
        finish(c)

    for copy in icopies[1:]:
        copy.wait_send()
    for k in range(4):
        x_copy(k).wait_send()
    for p in range(pieces):
        for d in range(n):
            for flag, make in q_moves(d):
                pl.when(flag)(lambda make=make: make(p, d).wait_send())
    for c in range(chunks):
        for d in range(1, n):
            stats_copy(c, d).wait_send()
            held = part.at[d, pl.ds(c * per_chunk, per_chunk)]
            remote(held, held, ps_sem.at[c, d], pr_sem.at[c, d], right).wait_send()


def local_kernel(tok_q, tok_kv, ref_kv, ref_ids):
    n = lax.axis_size("frames")
    frame_count, row_count, width = tok_q.shape
    heads = width // HEAD_DIM
    chunks, pieces = heads // 2, 2
    tokens = frame_count * row_count
    images, ref_rows = ref_kv.shape[1:3]
    span = 2 * ref_rows
    dma = pltpu.SemaphoreType.DMA
    in_hbm = pl.BlockSpec(memory_space=pltpu.HBM)
    return pl.pallas_call(
        functools.partial(kernel, n, chunks, pieces),
        out_shape=jax.ShapeDtypeStruct(tok_q.shape, jnp.bfloat16),
        in_specs=[in_hbm] * 3 + [pl.BlockSpec(memory_space=pltpu.SMEM)],
        out_specs=pl.BlockSpec(memory_space=pltpu.VMEM),
        scratch_shapes=[
            pltpu.VMEM((n,) + tok_q.shape, jnp.bfloat16),
            pltpu.VMEM((2,) + tok_kv.shape, jnp.bfloat16),
            pltpu.VMEM((2, images, span, width), jnp.bfloat16),
            pltpu.VMEM((n, 8, tokens), jnp.int32),
            pltpu.VMEM((heads, span, n * tokens), jnp.float32),
            pltpu.VMEM((heads, frame_count, 3 * tokens), jnp.float32),
            pltpu.VMEM((heads, 2 * row_count, tokens), jnp.float32),
            pltpu.VMEM((n, chunks, n, heads // chunks, 4, tokens), jnp.float32),
            pltpu.VMEM((heads, HEAD_DIM, images * span + 2 * tokens), jnp.bfloat16),
            pltpu.VMEM((n, heads, HEAD_DIM, tokens), jnp.float32),
            pltpu.VMEM((n, heads, HEAD_DIM, tokens), jnp.bfloat16),
            pltpu.VMEM((n + 1, heads, HEAD_DIM, tokens), jnp.bfloat16),
            dma((4,)),
            dma((4,)),
            dma((4,)),
            dma((pieces, n + 1)),
            dma((pieces, n)),
            dma((n,)),
            dma((n,)),
            dma((chunks, n)),
            dma((chunks, n)),
            dma((chunks, n)),
            dma((chunks, n + 1)),
        ],
        compiler_params=pltpu.CompilerParams(
            collective_id=0, has_side_effects=True, vmem_limit_bytes=64 * 1024 * 1024
        ),
    )(tok_q, tok_kv, ref_kv, ref_ids)


def local(tok_q, tok_kv, ref_kv, ref_ids):
    frame_count, row_count, width = tok_q.shape
    fits = (
        3 <= lax.axis_size("frames") <= 4
        and lax.axis_size("rows") == 2
        and frame_count == BAND
        and row_count % 16 == 0
        and frame_count * row_count == 128
        and ref_kv.shape[2] % 16 == 0
        and (width // HEAD_DIM) % 2 == 0
    )
    return (local_kernel if fits else local_general)(tok_q, tok_kv, ref_kv, ref_ids)


def solution(mesh):
    placed = (
        P(("clip", "frames"), "rows", "heads"),
        P(None, ("clip", "frames"), "rows", "heads"),
        P(None, "clip", ("frames", "rows"), "heads"),
        P(("clip", "frames")),
    )
    return jax.shard_map(
        local,
        mesh=mesh,
        in_specs=placed,
        out_specs=P(("clip", "frames"), "rows", "heads"),
        check_vma=False,
    )
```

```python
import functools

import jax
import jax.numpy as jnp
from jax import lax
from jax.experimental import pallas as pl
from jax.experimental.pallas import tpu as pltpu
from jax.sharding import PartitionSpec as P

HEAD_DIM = 128
BAND = 8


def padded_2(value, sides, width):
    for axis, dim in sides:
        devices, length = (lax.axis_size(axis), value.shape[dim])
        up = [(i, (i + 1) % devices) for i in range(devices)]
        down = [(j, i) for i, j in up]
        last = lax.slice_in_dim(value, length - width, length, axis=dim)
        first = lax.slice_in_dim(value, 0, width, axis=dim)
        before = lax.ppermute(last, axis, up)
        after = lax.ppermute(first, axis, down)
        value = jnp.concatenate([before, value, after], axis=dim)
    return value


def attend_frame(query, frame_keys, frame_values, image_keys, image_values, factor):
    local_scores = (
        jnp.einsum("thd,shd->hts", query, frame_keys, preferred_element_type=jnp.float32) * factor
    )
    image_scores = (
        jnp.einsum("thd,shd->hts", query, image_keys, preferred_element_type=jnp.float32) * factor
    )
    top = jnp.maximum(jnp.max(local_scores, axis=-1), jnp.max(image_scores, axis=-1))
    local_exp = jnp.exp(local_scores - top[..., None])
    image_exp = jnp.exp(image_scores - top[..., None])
    total = jnp.sum(local_exp, axis=-1) + jnp.sum(image_exp, axis=-1)
    local_weights = (local_exp / total[..., None]).astype(jnp.bfloat16)
    image_weights = (image_exp / total[..., None]).astype(jnp.bfloat16)
    result = jnp.einsum(
        "hts,shd->thd", local_weights, frame_values, preferred_element_type=jnp.float32
    )
    result = result + jnp.einsum(
        "hts,shd->thd", image_weights, image_values, preferred_element_type=jnp.float32
    )
    return result


def local_general(tok_q, tok_kv, ref_kv, ref_ids):
    frame_count, row_count, feat_width = tok_q.shape
    head_count = feat_width // HEAD_DIM
    factor = 1.0 / HEAD_DIM**0.5
    query_heads = tok_q.reshape(frame_count, row_count, head_count, HEAD_DIM)
    padded = padded_2(tok_kv, (("frames", 1),), BAND)
    band_scores = []
    for offset in range(2 * BAND + 1):
        key_block = padded[0, offset : offset + frame_count].reshape(
            frame_count, row_count, head_count, HEAD_DIM
        )
        band_scores.append(
            jnp.einsum("frhd,frhd->frh", query_heads, key_block, preferred_element_type=jnp.float32)
            * factor
        )
    band_weights = jax.nn.softmax(jnp.stack(band_scores), axis=0).astype(jnp.bfloat16)
    temporal = jnp.zeros((frame_count, row_count, head_count, HEAD_DIM), jnp.float32)
    for offset in range(2 * BAND + 1):
        value_block = padded[1, offset : offset + frame_count].reshape(
            frame_count, row_count, head_count, HEAD_DIM
        )
        temporal = temporal + jnp.einsum(
            "frh,frhd->frhd", band_weights[offset], value_block, preferred_element_type=jnp.float32
        )
    temporal = temporal.reshape(frame_count, row_count, feat_width)
    references = lax.all_gather(ref_kv, ("frames", "rows"), axis=2, tiled=True)
    ref_length = references.shape[2]

    def spatial_frame(inputs):
        query_frame, keys_frame, values_frame, image_id = inputs
        chosen = lax.dynamic_index_in_dim(references, image_id, axis=1, keepdims=False)
        image_keys = chosen[0].reshape(ref_length, head_count, HEAD_DIM)
        image_values = chosen[1].reshape(ref_length, head_count, HEAD_DIM)
        queries = query_frame.reshape(query_frame.shape[0], head_count, HEAD_DIM)
        keys_full = keys_frame.reshape(keys_frame.shape[0], head_count, HEAD_DIM)
        values_full = values_frame.reshape(values_frame.shape[0], head_count, HEAD_DIM)
        result = attend_frame(queries, keys_full, values_full, image_keys, image_values, factor)
        return result.reshape(query_frame.shape[0], feat_width)

    query_moved, pairs_moved = (
        lax.all_to_all(tok_q[None], "rows", split_axis=1, concat_axis=2, tiled=True),
        lax.all_to_all(tok_kv, "rows", split_axis=1, concat_axis=2, tiled=True),
    )
    per_device = frame_count // lax.axis_size("rows")
    local_ids = lax.dynamic_slice_in_dim(ref_ids, lax.axis_index("rows") * per_device, per_device)
    attended = lax.map(spatial_frame, (query_moved[0], pairs_moved[0], pairs_moved[1], local_ids))
    spatial = lax.all_to_all(attended, "rows", split_axis=1, concat_axis=0, tiled=True)
    return (temporal + spatial).astype(jnp.bfloat16)


NEG = -1e30
MESH = pl.DeviceIdType.MESH


def scores_of(keys, queries):
    return lax.dot_general(
        keys, queries, (((1,), (1,)), ((), ())), preferred_element_type=jnp.float32
    )


def kernel(
    n,
    chunks,
    q_hbm,
    kv_hbm,
    ref_hbm,
    ids_ref,
    out_ref,
    qbuf,
    kvbuf,
    rbuf,
    idbuf,
    pref,
    ptime,
    pframe,
    stats,
    vt,
    mine,
    part,
    got,
    local_sem,
    xs_sem,
    xr_sem,
    qs_sem,
    qr_sem,
    is_sem,
    ir_sem,
    ss_sem,
    sr_sem,
    ps_sem,
    pr_sem,
):
    frame_count, row_count, width = q_hbm.shape
    head_count = width // HEAD_DIM
    per_chunk = head_count // chunks
    chunk_width = per_chunk * HEAD_DIM
    tokens = frame_count * row_count
    images, ref_rows = ref_hbm.shape[1], ref_hbm.shape[2]
    span = 2 * ref_rows
    factor = 1.0 / HEAD_DIM**0.5
    me = lax.axis_index("frames")
    has_left, has_right = me >= 1, me <= n - 2
    middle = has_left & has_right
    across = {"rows": 1 - lax.axis_index("rows")}
    ahead = [{"frames": lax.rem(me + d, n)} for d in range(n)]
    right, left = ahead[1], ahead[n - 1]
    banded = (0, 1, n - 1)
    far_slots = list(range(2, n - 1))
    own_rows, far_rows = pl.ds(0, ref_rows), pl.ds(ref_rows, ref_rows)

    loads = [
        pltpu.make_async_copy(q_hbm, qbuf.at[0], local_sem.at[0]),
        pltpu.make_async_copy(ref_hbm.at[0], rbuf.at[0, :, own_rows], local_sem.at[1]),
        pltpu.make_async_copy(kv_hbm, kvbuf.at[0], local_sem.at[2]),
        pltpu.make_async_copy(ref_hbm.at[1], rbuf.at[1, :, own_rows], local_sem.at[3]),
    ]
    for copy in loads:
        copy.start()

    barrier = pltpu.get_barrier_semaphore()
    for d in range(1, n):
        pl.semaphore_signal(barrier, inc=1, device_id=ahead[d], device_id_type=MESH)
    pl.semaphore_signal(barrier, inc=1, device_id=across, device_id_type=MESH)

    lane_frame = lax.broadcasted_iota(jnp.int32, (8, tokens), 1) // row_count
    which = jnp.zeros((8, tokens), jnp.int32)
    for f in range(frame_count):
        which = jnp.where(lane_frame == f, ids_ref[f], which)
    idbuf[0] = which

    for copy in loads:
        copy.wait()
    pl.semaphore_wait(barrier, n)

    def remote(src, dst, send, recv, where):
        return pltpu.make_async_remote_copy(
            src_ref=src, dst_ref=dst, send_sem=send, recv_sem=recv,
            device_id=where, device_id_type=MESH,
        )

    def part_of(c):
        return pl.ds(c * chunk_width, chunk_width)

    def x_copy(c, k):
        cut = part_of(c)
        if k % 2 == 0:
            src, dst = rbuf.at[k // 2, :, own_rows, cut], rbuf.at[k // 2, :, far_rows, cut]
        else:
            src, dst = kvbuf.at[0, k // 2, :, :, cut], kvbuf.at[1, k // 2, :, :, cut]
        return remote(src, dst, xs_sem.at[c, k], xr_sem.at[c, k], across)

    def q_right(c, d):
        cut = part_of(c)
        src = qbuf.at[d, :, :, cut]
        return remote(
            src, qbuf.at[d + 1, :, :, cut], qs_sem.at[c, d], qr_sem.at[c, d + 1], right
        )

    def q_left(c, d):
        cut = part_of(c)
        src = qbuf.at[d, :, :, cut]
        to = (d if d else n) - 1
        return remote(
            src, qbuf.at[to, :, :, cut], qs_sem.at[c, d if d else n], qr_sem.at[c, to], left
        )

    def q_moves(d):
        if d == 0:
            return [(has_right, q_right), (has_left, q_left)]
        moves = []
        if d < n - 1:
            moves.append(((d <= me) & has_right, q_right))
        if d > 1:
            moves.append(((d > me) & has_left, q_left))
        return moves

    def send_queries(c, d):
        for flag, make in q_moves(d):
            pl.when(flag)(lambda make=make: make(c, d).start())

    def take_queries(c, d):
        cut = part_of(c)
        held = qbuf.at[d, :, :, cut]
        remote(held, held, qs_sem.at[c, d], qr_sem.at[c, d], right).wait_recv()
        send_queries(c, d)

    icopies = [None] + [
        remote(idbuf.at[0], idbuf.at[d], is_sem.at[d], ir_sem.at[d], ahead[d]) for d in range(1, n)
    ]
    for copy in icopies[1:]:
        copy.start()
    for c in range(chunks):
        send_queries(c, 0)
        for k in range(4):
            x_copy(c, k).start()

    slots = [n - 1, 0, 1] + far_slots
    banded_width, all_width = 3 * tokens, n * tokens
    here = slice(tokens, 2 * tokens)

    def grid(width, axis):
        return lax.broadcasted_iota(jnp.int32, (frame_count, row_count, width), axis)

    lane = lax.broadcasted_iota(jnp.int32, (1, banded_width), 1)
    lane_row, lane_block = lax.rem(lane, row_count), lax.div(lane, tokens)
    band_frame = lax.div(lax.rem(lane, tokens), row_count)
    lane_low = jnp.where(lane_block == 0, band_frame, 0)
    lane_high = jnp.where(lane_block == 2, band_frame, frame_count)

    def same_row(width):
        return grid(width, 1) == lane_row[None]

    def same_frame():
        return grid(tokens, 0) == band_frame[None, :, here]

    def in_band():
        keys = lax.broadcasted_iota(jnp.int32, (frame_count, banded_width), 0)
        return (keys >= lane_low) & (keys <= lane_high)

    def heads_of(c):
        return [(h, pl.ds(h * HEAD_DIM, HEAD_DIM)) for h in range(c * per_chunk, (c + 1) * per_chunk)]

    def side_by_side(rows):
        return jnp.concatenate(rows, axis=1)

    def score_block(c):
        chosen = side_by_side([idbuf[d][0:1] for d in slots])
        for h, cut in heads_of(c):
            query = jnp.concatenate(
                [qbuf[d, :, :, cut].reshape(tokens, HEAD_DIM) for d in slots], axis=0
            )
            image_keys = rbuf[0, :, :, cut].reshape(images * span, HEAD_DIM)
            both = scores_of(image_keys, query)
            score = both[0:span]
            for i in range(1, images):
                score = jnp.where(chosen == i, both[i * span : (i + 1) * span], score)
            score = score * factor
            keys = kvbuf[0, 0, :, :, cut].reshape(tokens, HEAD_DIM)
            near = scores_of(keys, query[0:banded_width]) * factor
            near = near.reshape(frame_count, row_count, banded_width)
            time = jnp.sum(jnp.where(same_row(banded_width), near, 0.0), axis=1)
            time = jnp.where(in_band(), time, NEG)
            time_top = jnp.max(time, axis=0, keepdims=True)
            time = jnp.exp(time - time_top)
            ptime[h] = time
            time_sum = jnp.sum(time, axis=0, keepdims=True)
            other_keys = kvbuf[1, 0, :, :, cut].reshape(tokens, HEAD_DIM)
            other = scores_of(other_keys, query[here]) * factor
            other = other.reshape(frame_count, row_count, tokens)
            frame = jnp.concatenate(
                [
                    jnp.sum(jnp.where(same_frame(), near[:, :, here], 0.0), axis=0),
                    jnp.sum(jnp.where(same_frame(), other, 0.0), axis=0),
                ],
                axis=0,
            )
            top = jnp.max(score, axis=0, keepdims=True)
            frame_top = jnp.max(frame, axis=0, keepdims=True)
            top = side_by_side(
                [
                    top[:, 0:tokens],
                    jnp.maximum(top[:, here], frame_top),
                    top[:, 2 * tokens :],
                ]
            )
            frame = jnp.exp(frame - top[:, here])
            pframe[h] = frame
            frame_sum = jnp.sum(frame, axis=0, keepdims=True)
            score = jnp.exp(score - top)
            pref[h] = score
            total = jnp.sum(score, axis=0, keepdims=True)
            for i, d in enumerate(slots):
                at = slice(i * tokens, (i + 1) * tokens)
                rows = [top[:, at], total[:, at] + frame_sum if d == 0 else total[:, at]]
                if d in banded:
                    rows += [time_top[:, at], time_sum[:, at]]
                else:
                    rows += [jnp.zeros((2, tokens), jnp.float32)]
                stats[0, c, d, h % per_chunk] = jnp.concatenate(rows, axis=0)

    def scale_of(c, d, h, k):
        tops, sums = [], []
        for e in range(n):
            place = (d - e) % n
            if k == 2 and place not in banded:
                continue
            block = stats[e, c, place, h % per_chunk]
            tops.append(block[k : k + 1])
            sums.append(block[k + 1 : k + 2])
        top = functools.reduce(jnp.maximum, tops)
        total = sum(s * jnp.exp(t - top) for t, s in zip(tops, sums))
        return jnp.exp(tops[0] - top) / total

    def value_block(c):
        chosen = side_by_side([idbuf[d][0:1] for d in slots])
        for h, cut in heads_of(c):
            scale = side_by_side([scale_of(c, d, h, 0) for d in slots])
            weight = pref[h] * scale
            weight = jnp.concatenate(
                [jnp.where(chosen == i, weight, 0.0).astype(jnp.bfloat16) for i in range(images)],
                axis=0,
            )
            start = images * span
            result = jnp.dot(vt[h, :, 0:start], weight, preferred_element_type=jnp.float32)
            time = ptime[h] * side_by_side([scale_of(c, d, h, 2) for d in slots[:3]])
            time = jnp.where(same_row(banded_width), time[:, None, :], 0.0)
            time = time.reshape(tokens, banded_width).astype(jnp.bfloat16)
            timed = jnp.dot(
                vt[h, :, start : start + tokens], time, preferred_element_type=jnp.float32
            )
            frame = pframe[h] * scale[:, here]
            frames = [
                jnp.where(same_frame(), frame[i * row_count : (i + 1) * row_count][None], 0.0)
                .reshape(tokens, tokens)
                .astype(jnp.bfloat16)
                for i in range(2)
            ]
            framed = jnp.dot(
                vt[h, :, start : start + 2 * tokens],
                jnp.concatenate(frames, axis=0),
                preferred_element_type=jnp.float32,
            )
            for i, d in enumerate(slots):
                at = slice(i * tokens, (i + 1) * tokens)
                piece = result[:, at]
                if d in banded:
                    piece = piece + timed[:, at]
                if d == 0:
                    piece = piece + framed
                mine[d, h] = piece

    def turn_values(c):
        for h, cut in heads_of(c):
            blocks = [
                rbuf[1, :, :, cut].reshape(images * span, HEAD_DIM),
                kvbuf[0, 1, :, :, cut].reshape(tokens, HEAD_DIM),
                kvbuf[1, 1, :, :, cut].reshape(tokens, HEAD_DIM),
            ]
            values = jnp.concatenate(blocks, axis=0).astype(jnp.float32)
            vt[h] = values.T.astype(jnp.bfloat16)

    def stats_copy(c, d):
        return remote(stats.at[0, c], stats.at[d, c], ss_sem.at[c, d], sr_sem.at[c, d], ahead[d])

    def p_left(c, d):
        held = pl.ds(c * per_chunk, per_chunk)
        return remote(
            part.at[d, held], got.at[d - 1, held], ps_sem.at[c, d], pr_sem.at[c, d - 1], left
        )

    def p_right(c, d):
        held = pl.ds(c * per_chunk, per_chunk)
        return remote(
            part.at[d, held], got.at[d + 1, held], ps_sem.at[c, d], pr_sem.at[c, d + 1], right
        )

    def p_wait(c, d):
        held = got.at[d, pl.ds(c * per_chunk, per_chunk)]
        remote(held, held, ps_sem.at[c, 0], pr_sem.at[c, d], right).wait_recv()

    def pass_on(c, d, gather):
        heads = [h for h, _ in heads_of(c)]
        if gather:
            p_wait(c, d)
        for h in heads:
            total = mine[d, h]
            if gather:
                total = total + got[d, h].astype(jnp.float32)
            part[d, h] = total.astype(jnp.bfloat16)
        pl.when(d <= me)(lambda: p_left(c, d).start())
        pl.when(d > me)(lambda: p_right(c, d).start())

    chain = far_slots + [n - 1, 1]

    def scores(c):
        for d in [1, n - 1] + far_slots:
            take_queries(c, d)
        x_copy(c, 0).wait_recv()
        x_copy(c, 1).wait_recv()
        score_block(c)
        for d in range(1, n):
            stats_copy(c, d).start()

    def values(c):
        x_copy(c, 2).wait_recv()
        x_copy(c, 3).wait_recv()
        turn_values(c)
        for d in range(1, n):
            stats_copy(c, d).wait_recv()
        value_block(c)

        @pl.when(jnp.logical_not(middle))
        def _():
            for d in chain:
                pass_on(c, d, False)

    def combine(c):
        @pl.when(middle)
        def _():
            for d in chain:
                pass_on(c, d, True)

    def finish(c):
        pl.when(has_right)(lambda: p_wait(c, 0))
        pl.when(has_left)(lambda: p_wait(c, n))
        for h, cut in heads_of(c):
            total = mine[0, h]
            total = total + jnp.where(has_right, got[0, h].astype(jnp.float32), 0.0)
            total = total + jnp.where(has_left, got[n, h].astype(jnp.float32), 0.0)
            out_ref[:, :, cut] = total.T.reshape(frame_count, row_count, HEAD_DIM).astype(
                jnp.bfloat16
            )

    got[0] = jnp.zeros_like(got[0])
    got[n] = jnp.zeros_like(got[n])
    for d in range(1, n):
        icopies[d].wait_recv()
    scores(0)
    for c in range(chunks):
        if c + 1 < chunks:
            scores(c + 1)
        if c >= 1:
            combine(c - 1)
        values(c)
    combine(chunks - 1)
    for c in range(chunks):
        finish(c)

    for copy in icopies[1:]:
        copy.wait_send()
    for c in range(chunks):
        for k in range(4):
            x_copy(c, k).wait_send()
        for d in range(n):
            for flag, make in q_moves(d):
                pl.when(flag)(lambda make=make: make(c, d).wait_send())
        for d in range(1, n):
            stats_copy(c, d).wait_send()
            held = part.at[d, pl.ds(c * per_chunk, per_chunk)]
            remote(held, held, ps_sem.at[c, d], pr_sem.at[c, d], right).wait_send()


def local_kernel(tok_q, tok_kv, ref_kv, ref_ids):
    n = lax.axis_size("frames")
    frame_count, row_count, width = tok_q.shape
    heads = width // HEAD_DIM
    chunks = heads // 2
    tokens = frame_count * row_count
    images, ref_rows = ref_kv.shape[1:3]
    span = 2 * ref_rows
    dma = pltpu.SemaphoreType.DMA
    in_hbm = pl.BlockSpec(memory_space=pltpu.HBM)
    return pl.pallas_call(
        functools.partial(kernel, n, chunks),
        out_shape=jax.ShapeDtypeStruct(tok_q.shape, jnp.bfloat16),
        in_specs=[in_hbm] * 3 + [pl.BlockSpec(memory_space=pltpu.SMEM)],
        out_specs=pl.BlockSpec(memory_space=pltpu.VMEM),
        scratch_shapes=[
            pltpu.VMEM((n,) + tok_q.shape, jnp.bfloat16),
            pltpu.VMEM((2,) + tok_kv.shape, jnp.bfloat16),
            pltpu.VMEM((2, images, span, width), jnp.bfloat16),
            pltpu.VMEM((n, 8, tokens), jnp.int32),
            pltpu.VMEM((heads, span, n * tokens), jnp.float32),
            pltpu.VMEM((heads, frame_count, 3 * tokens), jnp.float32),
            pltpu.VMEM((heads, 2 * row_count, tokens), jnp.float32),
            pltpu.VMEM((n, chunks, n, heads // chunks, 4, tokens), jnp.float32),
            pltpu.VMEM((heads, HEAD_DIM, images * span + 2 * tokens), jnp.bfloat16),
            pltpu.VMEM((n, heads, HEAD_DIM, tokens), jnp.float32),
            pltpu.VMEM((n, heads, HEAD_DIM, tokens), jnp.bfloat16),
            pltpu.VMEM((n + 1, heads, HEAD_DIM, tokens), jnp.bfloat16),
            dma((4,)),
            dma((chunks, 4)),
            dma((chunks, 4)),
            dma((chunks, n + 1)),
            dma((chunks, n)),
            dma((n,)),
            dma((n,)),
            dma((chunks, n)),
            dma((chunks, n)),
            dma((chunks, n)),
            dma((chunks, n + 1)),
        ],
        compiler_params=pltpu.CompilerParams(
            collective_id=0, has_side_effects=True, vmem_limit_bytes=64 * 1024 * 1024
        ),
    )(tok_q, tok_kv, ref_kv, ref_ids)


def local(tok_q, tok_kv, ref_kv, ref_ids):
    frame_count, row_count, width = tok_q.shape
    fits = (
        3 <= lax.axis_size("frames") <= 4
        and lax.axis_size("rows") == 2
        and frame_count == BAND
        and row_count % 16 == 0
        and frame_count * row_count == 128
        and ref_kv.shape[2] % 16 == 0
        and (width // HEAD_DIM) % 2 == 0
    )
    return (local_kernel if fits else local_general)(tok_q, tok_kv, ref_kv, ref_ids)


def solution(mesh):
    placed = (
        P(("clip", "frames"), "rows", "heads"),
        P(None, ("clip", "frames"), "rows", "heads"),
        P(None, "clip", ("frames", "rows"), "heads"),
        P(("clip", "frames")),
    )
    return jax.shard_map(
        local,
        mesh=mesh,
        in_specs=placed,
        out_specs=P(("clip", "frames"), "rows", "heads"),
        check_vma=False,
    )
```
